128 devices in a mesh: tm: 32 (over x, z, core), chan: 4 (over y).
Axes of the slice: x: 4, y: 4, z: 4, core: 2. Of those that a mesh axis runs over, the one named last changes fastest.
Arguments:
- record: float32 [32768, 1024], P('tm', 'chan'), may hold values from -120 to 120
- test_matrix: float32 [64, 1024, 128], P(None, 'chan'), may hold values from -0.0234375 to 0.0234375
Outputs:
- basis: float32 [32768, 128], P('tm')
- coeffs: float32 [64, 1024, 128], P('tm', 'chan')
The draws below stay inside these ranges and needn't reach their ends.
All inputs are finite; a program needn't handle non-finite values.
Results may differ from the reference program's by a relative error of at most 0.00024.
Values sent between devices are 32-bit elements; how exact they have to be, the bound alone decides.
A program may use at most 256 MiB of HBM per device.

```python
import jax
import jax.numpy as jnp
from jax import lax

C = 1024
L = 64
K = 128
NT = 32768


def draw_record(key, part):
    key_base = jax.random.fold_in(key, 11)
    key_chan = jax.random.fold_in(key, 12)
    steps = jnp.arange(NT, dtype=jnp.float32)
    ramp = 1.0 + 2.0 * steps / jnp.float32(max(NT - 1, 1))
    chan_scale = jnp.exp(jax.random.uniform(key_chan, (C,), jnp.float32, 0.0, 2.302585))
    base = jax.random.truncated_normal(key_base, -4.0, 4.0, (NT, C), jnp.float32)
    return (base * ramp[:, None] * chan_scale[None, :]).astype(jnp.float32)


def levels(own_key, extent, shards, least, largest):
    factor_of = 1.0
    for axis_at, blocks in shards:
        steps = jax.random.uniform(jax.random.fold_in(jax.random.fold_in(own_key, 6), axis_at), (blocks,), jnp.float32, least / len(shards), largest / len(shards))
        factor_of = factor_of * jnp.repeat(jnp.exp(steps), extent[axis_at] // blocks).reshape((-1,) + (1,) * (len(extent) - 1 - axis_at))
    return factor_of


def gaussian(stream_key, shape, deviation, bound, shards=(), held_as=jnp.bfloat16):
    entries = deviation * jax.random.normal(stream_key, shape, jnp.float32)
    if shards:
        entries = entries * levels(stream_key, shape, shards, -0.22, 0.18)
    return jnp.clip(entries, -bound, bound).astype(held_as)


def setup_inputs(seed: int = 0) -> dict:
    keys = jax.random.split(jax.random.key(seed), 3)
    record = draw_record(jax.random.fold_in(keys[2], 71), 0)
    test_matrix = gaussian(keys[1], (L, C, K), (C * L) ** -0.5, 0.0234375, ((1, 4),), jnp.float32)
    return dict(record=record, test_matrix=test_matrix)


def reference(record, test_matrix):
    hi = lax.Precision.HIGHEST
    padded = jnp.concatenate([record, jnp.zeros((L - 1, C), jnp.float32)], axis=0)
    sketch = jnp.zeros((NT, K), jnp.float32)
    for lag in range(L):
        sketch = sketch + jnp.dot(padded[lag:lag + NT].astype(jnp.float32), test_matrix[lag].astype(jnp.float32), precision=hi, preferred_element_type=jnp.float32)
    gram = jnp.dot(sketch.T.astype(jnp.float32), sketch.astype(jnp.float32), precision=hi, preferred_element_type=jnp.float32)
    lower = jnp.linalg.cholesky(gram)
    basis = lax.linalg.triangular_solve(lower, sketch, left_side=False, lower=True, transpose_a=True) * jnp.sqrt(jnp.float32(NT))
    scale = 1.0 / jnp.sqrt(jnp.float32(NT))
    coeffs = []
    for lag in range(L):
        coeffs.append(jnp.dot(padded[lag:lag + NT].T.astype(jnp.float32), basis.astype(jnp.float32), precision=hi, preferred_element_type=jnp.float32) * scale)
    return (basis, jnp.stack(coeffs, axis=0))
```

```python
import jax
import jax.numpy as jnp
from jax import lax
from jax.experimental import pallas as pl
from jax.experimental.pallas import tpu as pltpu
from jax.sharding import PartitionSpec as P

F32, BF16 = jnp.float32, jnp.bfloat16
MESH = pl.DeviceIdType.MESH
NX, NZ, NY = 4, 4, 4
LAGS, CH, K = 64, 256, 128
R = 1024
PR = 2 * R
A = 4
KC = 3 * A * CH
KT = 3 * PR + 128
NT_DOT = (((1,), (1,)), ((), ()))
TN_DOT = (((0,), (0,)), ((), ()))
HI = lax.Precision.HIGHEST


def halves(v):
    hi = v.astype(BF16)
    return hi, (v - hi.astype(F32)).astype(BF16)


def body(rec, w, basis_o, coef_o, xe, wf, xcat, rhs, yb, acc, ry, s_ext, xt, srhs, cp,
         xr, p1, pz, qz, q1, raw, gm, gx, gz, gb, gw, li, lsem, ss, rs):
    tm = lax.axis_index("tm")
    y = lax.axis_index("chan")
    h = tm % 2
    chip = tm // 2
    z = chip % NZ
    x = chip // NZ

    def at(xx, zz, hh):
        return (xx * NZ + zz) * 2 + hh

    sib = at(x, z, 1 - h)
    xn = [at((x + d) % NX, z, h) for d in range(NX)]
    zn = [at(x, (z + d) % NZ, h) for d in range(NZ)]
    yn = [(y + d) % NY for d in range(NY)]

    def send(src, dst, k, dt, dy):
        return pltpu.make_async_remote_copy(src_ref=src, dst_ref=dst, send_sem=ss.at[k], recv_sem=rs.at[k],
                                            device_id=(dt, dy), device_id_type=MESH)

    def arrived(ref, k):
        send(ref, ref, k, sib, y).wait_recv()

    count = [0]

    def sem():
        count[0] += 1
        return count[0] - 1

    own0 = pl.multiple_of(R * h, R)
    lx = pltpu.make_async_copy(rec, xe.at[pl.ds(own0, R)], lsem.at[0])
    lx.start()
    wcopies = []
    for p in range(8):
        for a in range(A):
            c = pltpu.make_async_copy(w.at[pl.ds(16 * a + 2 * p, 2)], wf.at[p, a], lsem.at[1 + 4 * p + a])
            c.start()
            wcopies.append(c)

    bar = pltpu.get_barrier_semaphore()

    def greet(dt, dy):
        pl.semaphore_signal(bar, inc=1, device_id=(dt, dy), device_id_type=MESH)

    greet(sib, y)
    for d in range(1, 4):
        greet(tm, yn[d])
        greet(sib, yn[d])
        greet(xn[d], y)
        greet(zn[d], y)
    gives = jnp.logical_and(h == 0, chip > 0)
    takes = chip < NX * NZ - 1
    down0, down1 = lax.max(tm - 2, 0), lax.max(tm - 1, 0)
    up = lax.min(2 * chip + 2, 2 * NX * NZ - 2)

    @pl.when(gives)
    def _():
        greet(down0, y)
        greet(down1, y)

    @pl.when(takes)
    def _():
        greet(up, y)

    pl.semaphore_wait(bar, 13 + jnp.where(gives, 2, 0) + jnp.where(takes, 1, 0))

    kh0, kh1, ks0, ks1 = sem(), sem(), sem(), sem()
    halo = xe.at[pl.ds(PR, 64)]
    heads = [send(rec.at[pl.ds(0, 64)], xe.at[pl.ds(own0, 64)], ks0, sib, y),
             send(rec.at[pl.ds(64, R - 64)], xe.at[pl.ds(pl.multiple_of(own0 + 64, 64), R - 64)], ks1, sib, y)]
    halos = [pltpu.make_async_remote_copy(src_ref=rec.at[pl.ds(0, 64)], dst_ref=halo, send_sem=ss.at[kk],
                                          recv_sem=rs.at[kh0], device_id=(dd, y), device_id_type=MESH)
             for kk, dd in ((kh0, down0), (kh1, down1))]
    heads[0].start()

    @pl.when(gives)
    def _():
        halos[0].start()
        halos[1].start()

    heads[1].start()

    def prep_w(p, slot):
        for a in range(A):
            for j in range(2):
                hi, lo = halves(wf[p, a, j])
                cs = pl.ds(128 * j, 128)
                rhs[slot, pl.ds(a * CH, CH), cs] = hi
                rhs[slot, pl.ds((A + a) * CH, CH), cs] = lo
                rhs[slot, pl.ds((2 * A + a) * CH, CH), cs] = hi

    for c in wcopies[:4]:
        c.wait()
    prep_w(0, 0)
    acc[...] = jnp.zeros_like(acc)
    zpad = jnp.zeros((16, K), F32)
    s_ext[pl.ds(0, 16)] = zpad
    s_ext[pl.ds(16 + PR, 16)] = zpad
    lx.wait()
    oth0 = pl.multiple_of(R - R * h, R)

    @pl.when(jnp.logical_not(takes))
    def _():
        halo[...] = jnp.zeros((64, CH), F32)

    @pl.when(takes)
    def _():
        arrived(halo, kh0)

    arrived(xe.at[pl.ds(oth0, 64)], ks0)

    @pl.loop(0, 13)
    def _(i):
        for a in range(A):
            hi, lo = halves(xe[pl.ds(pl.multiple_of(R * h + 80 * i + 16 * a, 16), 80), :])
            rows = pl.ds(pl.multiple_of(80 * i, 16), 80)
            xcat[rows, pl.ds(a * CH, CH)] = hi
            xcat[rows, pl.ds((A + a) * CH, CH)] = hi
            xcat[rows, pl.ds((2 * A + a) * CH, CH)] = lo

    for c in wcopies[4:]:
        c.wait()

    @pl.loop(0, 8)
    def _(p):
        slot = p % 2
        res = jnp.dot(xcat[...], rhs[slot], preferred_element_type=F32)
        yb[0] = res[:, :K]
        yb[1] = res[:, K:]
        prep_w(lax.min(p + 1, 7), 1 - slot)
        acc[...] += yb[0, pl.ds(2 * p, R), :] + yb[1, pl.ds(2 * p + 1, R), :]

    kry = [sem() for _ in range(3)]
    outs = []
    for d in (2, 1, 3):
        c = send(acc.at[pl.ds(pl.multiple_of(yn[d] * 256, 256), 256)], ry.at[d - 1], kry[d - 1], tm, yn[d])
        c.start()
        outs.append(c)
    arrived(xe.at[pl.ds(pl.multiple_of(oth0 + 64, 64), R - 64)], ks1)

    def xprep(i):
        cols = pl.multiple_of(128 * i, 128)
        for a in range(A):
            v = xe[pl.ds(pl.multiple_of(128 * i + 16 * a, 16), 128), :].T
            hi, lo = halves(v)
            rows = pl.ds(a * CH, CH)
            xt[rows, pl.ds(cols, 128)] = hi
            xt[rows, pl.ds(pl.multiple_of(PR + cols, 128), 128)] = hi
            xt[rows, pl.ds(pl.multiple_of(2 * PR + cols, 128), 128)] = lo

    for a in range(A):
        v = xe[pl.ds(PR + 16 * a, 16), :]
        hi = v.astype(BF16).astype(F32)
        t = jnp.concatenate([hi, hi, v - hi, jnp.zeros((80, CH), F32)], axis=0)
        xt[pl.ds(a * CH, CH), pl.ds(3 * PR, 128)] = t.T.astype(BF16)
    pl.loop(0, 8)(xprep)
    for d in range(1, 4):
        arrived(ry.at[d - 1], kry[d - 1])
    own_q = pl.ds(pl.multiple_of(y * 256, 256), 256)
    mine = pl.ds(pl.multiple_of(16 + R * h + 256 * y, 16), 256)
    s_ext[mine] = (acc[own_q] + ry[0]) + (ry[1] + ry[2])

    kag = [sem() for _ in range(3)]
    kfw = [sem() for _ in range(4)]

    def place(hh, yy):
        return s_ext.at[pl.ds(pl.multiple_of(16 + R * hh + 256 * yy, 16), 256)]

    for d in (2, 1, 3):
        c = send(place(h, y), place(h, y), kag[d - 1], tm, yn[d])
        c.start()
        outs.append(c)
    c = send(place(h, y), place(h, y), kfw[0], sib, y)
    c.start()
    outs.append(c)
    pl.loop(8, 16)(xprep)
    for d in (1, 3, 2):
        src = place(h, (y + 4 - d) % NY)
        arrived(src, kag[d - 1])
        c = send(src, src, kfw[d], sib, y)
        c.start()
        outs.append(c)
    for d in range(4):
        arrived(place(1 - h, (y + 4 - d) % NY), kfw[d])

    def prep_s(b0, slot):
        for j in range(2):
            cs = pl.ds(128 * j, 128)

            @pl.loop(0, 16)
            def _(i):
                hi, lo = halves(s_ext[pl.ds(128 * i + 16 - b0 - j, 128), :])
                o = pl.multiple_of(128 * i, 128)
                srhs[slot, pl.ds(o, 128), cs] = hi
                srhs[slot, pl.ds(pl.multiple_of(PR + o, 128), 128), cs] = lo
                srhs[slot, pl.ds(pl.multiple_of(2 * PR + o, 128), 128), cs] = hi

            v = s_ext[pl.ds(PR + 16 - b0 - j, 16), :]
            hi, lo = halves(v)
            srhs[slot, pl.ds(3 * PR, 16), cs] = hi
            srhs[slot, pl.ds(3 * PR + 16, 16), cs] = lo
            srhs[slot, pl.ds(3 * PR + 32, 16), cs] = hi
            srhs[slot, pl.ds(3 * PR + 48, 80), cs] = jnp.zeros((80, K), BF16)

    order = (2, 1, 3, 0)

    def tile(t, zd):
        prep_s(4 * zd + 2 * h, 0)
        for half in range(2):
            rows = pl.ds(512 * half, 512)
            res = jnp.dot(xt[rows, :], srhs[0], preferred_element_type=F32)
            cp[t, 0, rows, :] = res[:, :K]
            cp[t, 1, rows, :] = res[:, K:]

    def blk(i, ab=None):
        if ab is None:
            return pl.ds(pl.multiple_of(i * CH, CH), CH)
        return pl.ds(pl.multiple_of(i * CH + 128 * ab, 128), 128)

    xk = [[sem() for _ in range(6)] for _ in range(5)]
    xp, xm, xo = (x + 1) % 4, (x + 3) % 4, (x + 2) % 4

    def go(src, dst, k, dt):
        c = send(src, dst, k, dt, y)
        c.start()
        outs.append(c)

    def x_first(n, src):
        go(src.at[blk(xo, 0)], xr.at[n, 0], xk[n][0], xn[1])
        go(src.at[blk(xo, 1)], xr.at[n, 1], xk[n][1], xn[3])
        go(src.at[blk(xm, 0)], xr.at[n, 2], xk[n][2], xn[3])
        go(src.at[blk(xp, 1)], xr.at[n, 3], xk[n][3], xn[1])

    def x_second(n, src):
        arrived(xr.at[n, 0], xk[n][0])
        src[blk(xp, 0)] += xr[n, 0]
        go(src.at[blk(xp, 0)], xr.at[n, 4], xk[n][4], xn[1])
        arrived(xr.at[n, 1], xk[n][1])
        src[blk(xm, 1)] += xr[n, 1]
        go(src.at[blk(xm, 1)], xr.at[n, 5], xk[n][5], xn[3])

    def x_last(n, src, dst):
        arrived(xr.at[n, 2], xk[n][2])
        arrived(xr.at[n, 3], xk[n][3])
        arrived(xr.at[n, 4], xk[n][4])
        arrived(xr.at[n, 5], xk[n][5])
        dst[0:128] = src[blk(x, 0)] + (xr[n, 2] + xr[n, 4])
        dst[128:256] = src[blk(x, 1)] + (xr[n, 3] + xr[n, 5])

    zk = [[sem() for _ in range(6)] for _ in range(2)]

    def z_part(t, src, buf, ks, dst=None):
        half = buf.shape[1]
        a, b = pl.ds(0, half), pl.ds(half, half)
        if t == 0:
            go(src.at[a], buf.at[0], ks[0], zn[1])
            go(src.at[b], buf.at[1], ks[1], zn[3])
        elif t == 1:
            go(src.at[b], buf.at[3], ks[3], zn[1])
            arrived(buf.at[0], ks[0])
            src[a] += buf[0]
            go(src.at[a], buf.at[4], ks[4], zn[1])
        elif t == 2:
            go(src.at[a], buf.at[2], ks[2], zn[3])
            arrived(buf.at[1], ks[1])
            src[b] += buf[1]
            go(src.at[b], buf.at[5], ks[5], zn[3])
        else:
            for i in (2, 3, 4, 5):
                arrived(buf.at[i], ks[i])
            dst[a] = src[a] + (buf[2] + buf[4])
            dst[b] = src[b] + (buf[3] + buf[5])

    kgx = [sem() for _ in range(3)]
    kgz = [sem() for _ in range(3)]
    kgb = [sem() for _ in range(7)]
    piece = pl.ds(pl.multiple_of((h * NY + y) * 16, 16), 16)

    def zdest(t):
        return (z + order[t]) % NZ

    def pt(t):
        return cp.at[t, 0]

    def qt(t):
        return cp.at[t, 1]

    tile(0, zdest(0))
    x_first(0, pt(0))
    z_part(0, qt(0), qz, zk[1])
    sv = s_ext[pl.ds(16, PR), :]
    gm[...] = lax.dot_general(sv, sv, TN_DOT, precision=HI, preferred_element_type=F32)
    for d in range(1, 4):
        go(gm.at[piece], gx.at[d - 1], kgx[d - 1], xn[d])
    tile(1, zdest(1))
    z_part(1, qt(1), qz, zk[1])
    x_first(1, pt(1))
    x_second(0, pt(0))
    for d in range(1, 4):
        arrived(gx.at[d - 1], kgx[d - 1])
    gz[3] = sum_in_order(gm[piece], gx, x)
    for d in range(1, 4):
        go(gz.at[3], gz.at[d - 1], kgz[d - 1], zn[d])
    tile(2, zdest(2))
    z_part(2, qt(2), qz, zk[1])
    x_first(2, pt(2))
    x_second(1, pt(1))
    x_last(0, pt(0), p1.at[0])
    z_part(0, p1.at[0], pz, zk[0])
    for d in range(1, 4):
        arrived(gz.at[d - 1], kgz[d - 1])
    gb[piece] = sum_in_order(gz[3], gz, z)
    for i, (dt, dy) in enumerate([(tm, yn[1]), (tm, yn[2]), (tm, yn[3]), (sib, y), (sib, yn[1]), (sib, yn[2]), (sib, yn[3])]):
        c = send(gb.at[piece], gb.at[piece], kgb[i], dt, dy)
        c.start()
        outs.append(c)
    tile(3, zdest(3))
    x_first(3, pt(3))
    x_second(2, pt(2))
    z_part(3, qt(3), qz, zk[1], q1)
    x_first(4, q1)
    x_last(1, pt(1), p1.at[1])
    z_part(1, p1.at[1], pz, zk[0])
    x_second(3, pt(3))
    for i in range(7):
        d = (0, 1, 2, 3)[(i + 1) % 4] if i < 3 else i - 3
        hh = h if i < 3 else 1 - h
        arrived(gb.at[pl.ds(pl.multiple_of((hh * NY + (y + 4 - d) % NY) * 16, 16), 16)], kgb[i])
    gw[...] = gb[...]
    factor(gw, li)
    x_last(2, pt(2), p1.at[2])
    z_part(2, p1.at[2], pz, zk[0])
    x_second(4, q1)
    root = float(NX * NZ * PR) ** 0.5
    own_s = s_ext[pl.ds(pl.multiple_of(16 + R * h, 16), R), :]
    basis_o[...] = lax.dot_general(own_s, li[...], NT_DOT, precision=HI, preferred_element_type=F32) * root
    x_last(3, pt(3), p1.at[3])
    z_part(3, p1.at[3], pz, zk[0], raw.at[0])
    x_last(4, q1, raw.at[1])
    for j in range(2):
        coef_o[j] = lax.dot_general(raw[j], li[...], NT_DOT, precision=HI, preferred_element_type=F32)

    for c in outs:
        c.wait_send()
    heads[0].wait_send()
    heads[1].wait_send()

    @pl.when(gives)
    def _():
        halos[0].wait_send()
        halos[1].wait_send()


def sum_in_order(own, bufs, me):
    total = None
    for pos in range(4):
        v = jnp.where(me == pos, own, jnp.zeros_like(own))
        for d in range(1, 4):
            v = v + jnp.where((me + 4 - d) % 4 == pos, bufs[d - 1], jnp.zeros_like(own))
        total = v if total is None else total + v
    return total


def factor(g, li):
    rows = lax.broadcasted_iota(jnp.int32, (K, K), 0)
    cols = lax.broadcasted_iota(jnp.int32, (K, K), 1)
    li[...] = jnp.where(rows == cols, 1.0, 0.0).astype(F32)

    @pl.loop(0, K // 8)
    def _(jb):
        base = pl.multiple_of(jb * 8, 8)
        for j in range(8):
            pa = g[pl.ds(base, 8), :][j : j + 1, :]
            pb = li[pl.ds(base, 8), :][j : j + 1, :]
            r = lax.rsqrt(pa[:, j : j + 1])
            ra = pa * r
            rb = pb * r
            av = g[...]
            f = jnp.where(rows[:, :1] > base + j, av[:, j : j + 1] * r, 0.0)
            g[...] = av - f * ra
            li[...] = jnp.where(rows == base + j, rb, li[...] - f * rb)
        g[...] = pltpu.roll(g[...], K - 8, 1)


N_SEM = 4 + 3 + 3 + 4 + 30 + 12 + 3 + 3 + 7


def on_device(record, test_matrix):
    V = pl.BlockSpec(memory_space=pltpu.VMEM)
    H = pl.BlockSpec(memory_space=pl.ANY)
    return pl.pallas_call(
        body,
        out_shape=(jax.ShapeDtypeStruct((R, K), F32), jax.ShapeDtypeStruct((2, CH, K), F32)),
        in_specs=[H, H],
        out_specs=(V, V),
        scratch_shapes=[
            pltpu.VMEM((PR + 64, CH), F32),
            pltpu.VMEM((8, A, 2, CH, K), F32),
            pltpu.VMEM((R + 16, KC), BF16),
            pltpu.VMEM((2, KC, 2 * K), BF16),
            pltpu.VMEM((2, R + 16, K), F32),
            pltpu.VMEM((R, K), F32),
            pltpu.VMEM((3, 256, K), F32),
            pltpu.VMEM((PR + 32, K), F32),
            pltpu.VMEM((A * CH, KT), BF16),
            pltpu.VMEM((1, KT, 2 * K), BF16),
            pltpu.VMEM((4, 2, A * CH, K), F32),
            pltpu.VMEM((5, 6, 128, K), F32),
            pltpu.VMEM((4, CH, K), F32),
            pltpu.VMEM((6, 128, K), F32),
            pltpu.VMEM((6, 512, K), F32),
            pltpu.VMEM((A * CH, K), F32),
            pltpu.VMEM((2, CH, K), F32),
            pltpu.VMEM((K, K), F32),
            pltpu.VMEM((3, 16, K), F32),
            pltpu.VMEM((4, 16, K), F32),
            pltpu.VMEM((K, K), F32),
            pltpu.VMEM((K, K), F32),
            pltpu.VMEM((K, K), F32),
            pltpu.SemaphoreType.DMA((33,)),
            pltpu.SemaphoreType.DMA((N_SEM,)),
            pltpu.SemaphoreType.DMA((N_SEM,)),
        ],
        compiler_params=pltpu.CompilerParams(collective_id=0, has_side_effects=True, vmem_limit_bytes=60 * 2**20),
    )(record, test_matrix)


def solution(mesh):
    return jax.shard_map(
        on_device,
        mesh=mesh,
        in_specs=(P("tm", "chan"), P(None, "chan", None)),
        out_specs=(P("tm", None), P("tm", "chan", None)),
        check_vma=False,
    )
```

```python
import jax
import jax.numpy as jnp
from jax import lax
from jax.experimental import pallas as pl
from jax.experimental.pallas import tpu as pltpu
from jax.sharding import PartitionSpec as P

F32, BF16 = jnp.float32, jnp.bfloat16
MESH = pl.DeviceIdType.MESH
NX, NZ, NY = 4, 4, 4
LAGS, CH, K = 64, 256, 128
R = 1024
PR = 2 * R
A = 4
KC = 3 * A * CH
KT = 3 * PR + 128
NT_DOT = (((1,), (1,)), ((), ()))
TN_DOT = (((0,), (0,)), ((), ()))
HI = lax.Precision.HIGHEST


def halves(v):
    hi = v.astype(BF16)
    return hi, (v - hi.astype(F32)).astype(BF16)


def body(rec, w, basis_o, coef_o, xe, wf, xcat, rhs, yb, acc, ry, s_ext, xt, srhs, cp,
         xr, p1, q1, pz, qz, raw, gm, ge, gx, gz, gb, gw, li, lsem, ss, rs):
    tm = lax.axis_index("tm")
    y = lax.axis_index("chan")
    h = tm % 2
    chip = tm // 2
    z = chip % NZ
    x = chip // NZ

    def at(xx, zz, hh):
        return (xx * NZ + zz) * 2 + hh

    sib = at(x, z, 1 - h)
    xn = [at((x + d) % NX, z, h) for d in range(NX)]
    zn = [at(x, (z + d) % NZ, h) for d in range(NZ)]
    yn = [(y + d) % NY for d in range(NY)]

    def send(src, dst, k, dt, dy):
        return pltpu.make_async_remote_copy(src_ref=src, dst_ref=dst, send_sem=ss.at[k], recv_sem=rs.at[k],
                                            device_id=(dt, dy), device_id_type=MESH)

    def arrived(ref, k):
        send(ref, ref, k, sib, y).wait_recv()

    count = [0]

    def sem():
        count[0] += 1
        return count[0] - 1

    own0 = pl.multiple_of(R * h, R)
    lx = pltpu.make_async_copy(rec, xe.at[pl.ds(own0, R)], lsem.at[0])
    lx.start()
    wcopies = []
    for p in range(8):
        for a in range(A):
            c = pltpu.make_async_copy(w.at[pl.ds(16 * a + 2 * p, 2)], wf.at[p, a], lsem.at[1 + 4 * p + a])
            c.start()
            wcopies.append(c)

    bar = pltpu.get_barrier_semaphore()

    def greet(dt, dy):
        pl.semaphore_signal(bar, inc=1, device_id=(dt, dy), device_id_type=MESH)

    greet(sib, y)
    for d in range(1, 4):
        greet(tm, yn[d])
        greet(sib, yn[d])
        greet(xn[d], y)
        greet(zn[d], y)
    gives = jnp.logical_and(h == 0, chip > 0)
    takes = chip < NX * NZ - 1
    down0, down1 = lax.max(tm - 2, 0), lax.max(tm - 1, 0)
    up = lax.min(2 * chip + 2, 2 * NX * NZ - 2)

    @pl.when(gives)
    def _():
        greet(down0, y)
        greet(down1, y)

    @pl.when(takes)
    def _():
        greet(up, y)

    def prep_w(p, slot):
        for a in range(A):
            for j in range(2):
                hi, lo = halves(wf[p, a, j])
                cs = pl.ds(128 * j, 128)
                rhs[slot, pl.ds(a * CH, CH), cs] = hi
                rhs[slot, pl.ds((A + a) * CH, CH), cs] = lo
                rhs[slot, pl.ds((2 * A + a) * CH, CH), cs] = hi

    def prep_x(i):
        for a in range(A):
            hi, lo = halves(xe[pl.ds(pl.multiple_of(R * h + 80 * i + 16 * a, 16), 80), :])
            rows = pl.ds(pl.multiple_of(80 * i, 16), 80)
            xcat[rows, pl.ds(a * CH, CH)] = hi
            xcat[rows, pl.ds((A + a) * CH, CH)] = hi
            xcat[rows, pl.ds((2 * A + a) * CH, CH)] = lo

    acc[...] = jnp.zeros_like(acc)
    zpad = jnp.zeros((16, K), F32)
    s_ext[pl.ds(0, 16)] = zpad
    s_ext[pl.ds(16 + PR, 16)] = zpad
    lx.wait()
    pl.loop(0, 12)(prep_x)
    for c in wcopies[:4]:
        c.wait()
    prep_w(0, 0)
    pl.semaphore_wait(bar, 13 + jnp.where(gives, 2, 0) + jnp.where(takes, 1, 0))

    kh0, kh1, ks0, ks1 = sem(), sem(), sem(), sem()
    halo = xe.at[pl.ds(PR, 64)]
    heads = [send(rec.at[pl.ds(0, 64)], xe.at[pl.ds(own0, 64)], ks0, sib, y),
             send(rec.at[pl.ds(64, R - 64)], xe.at[pl.ds(pl.multiple_of(own0 + 64, 64), R - 64)], ks1, sib, y)]
    halos = [pltpu.make_async_remote_copy(src_ref=rec.at[pl.ds(0, 64)], dst_ref=halo, send_sem=ss.at[kk],
                                          recv_sem=rs.at[kh0], device_id=(dd, y), device_id_type=MESH)
             for kk, dd in ((kh0, down0), (kh1, down1))]

    @pl.when(gives)
    def _():
        halos[0].start()
        halos[1].start()

    heads[0].start()
    heads[1].start()
    for c in wcopies[4:]:
        c.wait()
    oth0 = pl.multiple_of(R - R * h, R)
    outs = []

    def go(src, dst, k, dt, dy=y):
        c = send(src, dst, k, dt, dy)
        c.start()
        outs.append(c)

    kry = [sem() for _ in range(3)]
    ycopies = {d: send(acc.at[pl.ds(pl.multiple_of(yn[d] * 256, 256), 256)], ry.at[d - 1], kry[d - 1], tm, yn[d])
               for d in (2, 1, 3)}
    HR = R // 2
    for half in range(2):
        if half == 1:
            @pl.when(jnp.logical_not(takes))
            def _():
                halo[...] = jnp.zeros((64, CH), F32)

            @pl.when(takes)
            def _():
                arrived(halo, kh0)

            arrived(xe.at[pl.ds(oth0, 64)], ks0)
            prep_x(12)

        @pl.loop(0, 8)
        def _(p):
            slot = p % 2
            res = jnp.dot(xcat[pl.ds(HR * half, HR + 16)], rhs[slot], preferred_element_type=F32)
            yb[0] = res[:, :K]
            yb[1] = res[:, K:]
            prep_w((p + 1) % 8, 1 - slot)
            acc[pl.ds(HR * half, HR)] += yb[0, pl.ds(2 * p, HR), :] + yb[1, pl.ds(2 * p + 1, HR), :]

        for d in (2, 1, 3):
            pl.when(yn[d] // 2 == half)(ycopies[d].start)
    outs.extend(ycopies.values())
    arrived(xe.at[pl.ds(pl.multiple_of(oth0 + 64, 64), R - 64)], ks1)

    order = (2, 1, 3, 0)
    shift = [16 * ((x + o) % 4) for o in order]

    def xprep(i):
        cols = pl.multiple_of(128 * i, 128)
        for a in range(A):
            v = xe[pl.ds(pl.multiple_of(128 * i + shift[a], 16), 128), :].T
            hi, lo = halves(v)
            rows = pl.ds(a * CH, CH)
            xt[rows, pl.ds(cols, 128)] = hi
            xt[rows, pl.ds(pl.multiple_of(PR + cols, 128), 128)] = hi
            xt[rows, pl.ds(pl.multiple_of(2 * PR + cols, 128), 128)] = lo

    for a in range(A):
        v = xe[pl.ds(pl.multiple_of(PR + shift[a], 16), 16), :]
        hi = v.astype(BF16).astype(F32)
        t = jnp.concatenate([hi, hi, v - hi, jnp.zeros((80, CH), F32)], axis=0)
        xt[pl.ds(a * CH, CH), pl.ds(3 * PR, 128)] = t.T.astype(BF16)
    pl.loop(0, 8)(xprep)
    for d in range(1, 4):
        arrived(ry.at[d - 1], kry[d - 1])
    own_q = pl.ds(pl.multiple_of(y * 256, 256), 256)
    mine = pl.ds(pl.multiple_of(16 + R * h + 256 * y, 16), 256)
    s_ext[mine] = (acc[own_q] + ry[0]) + (ry[1] + ry[2])

    kag = [sem() for _ in range(3)]
    kfw = [sem() for _ in range(4)]
    kge = [sem() for _ in range(7)]
    kgx = [sem() for _ in range(3)]
    kgz = [sem() for _ in range(3)]
    kgb = [sem() for _ in range(7)]

    def place(hh, yy):
        return s_ext.at[pl.ds(pl.multiple_of(16 + R * hh + 256 * yy, 16), 256)]

    def piece(hh, yy):
        return pl.ds(pl.multiple_of((hh * NY + yy) * 16, 16), 16)

    for d in (2, 1, 3):
        go(place(h, y), place(h, y), kag[d - 1], tm, yn[d])
    go(place(h, y), place(h, y), kfw[0], sib)
    sv = s_ext[mine]
    gm[...] = lax.dot_general(sv, sv, TN_DOT, precision=HI, preferred_element_type=F32)
    eight = [(0, 1), (0, 2), (0, 3), (1, 0), (1, 1), (1, 2), (1, 3)]
    hs, ts = (h, 1 - h), (tm, sib)
    for i, (o, d) in enumerate(eight):
        go(gm.at[piece(hs[o], yn[d])], ge.at[i], kge[i], ts[o], yn[d])
    pl.loop(8, 16)(xprep)
    for i in range(7):
        arrived(ge.at[i], kge[i])
    gm[piece(h, y)] = (((gm[piece(h, y)] + ge[0]) + (ge[1] + ge[2])) + ((ge[3] + ge[4]) + (ge[5] + ge[6])))
    for d in range(1, 4):
        go(gm.at[piece(h, y)], gx.at[d - 1], kgx[d - 1], xn[d])
    for d in (1, 3, 2):
        src = place(h, (y + 4 - d) % NY)
        arrived(src, kag[d - 1])
        go(src, src, kfw[d], sib)
    for d in range(1, 4):
        arrived(gx.at[d - 1], kgx[d - 1])
    gz[3] = (gm[piece(h, y)] + gx[0]) + (gx[1] + gx[2])
    for d in range(1, 4):
        go(gz.at[3], gz.at[d - 1], kgz[d - 1], zn[d])
    for d in range(4):
        arrived(place(1 - h, (y + 4 - d) % NY), kfw[d])

    def prep_s(n, j, pair):
        for c in range(2):
            cs = pl.ds(128 * c, 128)
            off = 16 - j - 2 * h - 4 * ((z + order[2 * pair + c]) % NZ)
            hi, lo = halves(s_ext[pl.ds(off, PR), :])
            srhs[n, pl.ds(0, PR), cs] = hi
            srhs[n, pl.ds(PR, PR), cs] = lo
            srhs[n, pl.ds(2 * PR, PR), cs] = hi
            hi, lo = halves(s_ext[pl.ds(PR + off, 16), :])
            srhs[n, pl.ds(3 * PR, 16), cs] = hi
            srhs[n, pl.ds(3 * PR + 16, 16), cs] = lo
            srhs[n, pl.ds(3 * PR + 32, 16), cs] = hi
            srhs[n, pl.ds(3 * PR + 48, 80), cs] = jnp.zeros((80, K), BF16)

    def unit_p(t, u):
        rows = pl.ds(512 * u, 512)
        res = jnp.dot(xt[rows, :], srhs[t], preferred_element_type=F32)
        for c in range(2):
            cp[2 * t + c, rows, :] = res[:, 128 * c : 128 * c + 128]

    def unit_q(t, u):
        res = jnp.dot(xt[pl.ds(512 * t, 512), :], srhs[2 + u], preferred_element_type=F32)
        for m in range(2):
            for c in range(2):
                cp[4 + 2 * t + m, pl.ds(256 * (2 * u + c), 256), :] = res[256 * m : 256 * m + 256, 128 * c : 128 * c + 128]

    rk = [[sem() for _ in range(6)] for _ in range(8)]

    def ends(n):
        return (xn[1], xn[3]) if n < 4 else (zn[1], zn[3])

    def first(n, u):
        up, dn = ends(n)
        src, buf = cp.at[n], xr.at[n]
        if u == 0:
            go(src.at[0:128], buf.at[0], rk[n][0], up)
            go(src.at[128:256], buf.at[1], rk[n][1], dn)
            go(src.at[384:512], buf.at[3], rk[n][3], up)
        else:
            go(src.at[512:640], buf.at[2], rk[n][2], dn)

    def second(n):
        up, dn = ends(n)
        arrived(xr.at[n, 0], rk[n][0])
        cp[n, 256:384] += xr[n, 0]
        go(cp.at[n, 256:384], xr.at[n, 4], rk[n][4], up)
        arrived(xr.at[n, 1], rk[n][1])
        cp[n, 640:768] += xr[n, 1]
        go(cp.at[n, 640:768], xr.at[n, 5], rk[n][5], dn)

    def last(n, dst):
        for i in (2, 3, 4, 5):
            arrived(xr.at[n, i], rk[n][i])
        dst[0:128] = cp[n, 768:896] + (xr[n, 2] + xr[n, 4])
        dst[128:256] = cp[n, 896:1024] + (xr[n, 3] + xr[n, 5])

    zk = [[sem() for _ in range(6)] for _ in range(2)]

    def part(q, t, src, dst=None):
        up, dn = ends(0 if q else 4)
        buf, ks = (pz, qz)[q], zk[q]
        a, b = pl.ds(0, 128), pl.ds(128, 128)
        if t == 0:
            go(src.at[a], buf.at[0], ks[0], up)
            go(src.at[b], buf.at[1], ks[1], dn)
        elif t == 1:
            go(src.at[b], buf.at[3], ks[3], up)
            arrived(buf.at[0], ks[0])
            src[a] += buf[0]
            go(src.at[a], buf.at[4], ks[4], up)
        elif t == 2:
            go(src.at[a], buf.at[2], ks[2], dn)
            arrived(buf.at[1], ks[1])
            src[b] += buf[1]
            go(src.at[b], buf.at[5], ks[5], dn)
        else:
            for i in (2, 3, 4, 5):
                arrived(buf.at[i], ks[i])
            dst[a] = src[a] + (buf[2] + buf[4])
            dst[b] = src[b] + (buf[3] + buf[5])

    prep_s(0, 0, 0)
    unit_p(0, 0)
    first(0, 0)
    first(1, 0)
    for d in range(1, 4):
        arrived(gz.at[d - 1], kgz[d - 1])
    gb[piece(h, y)] = (gz[3] + gz[0]) + (gz[1] + gz[2])
    for i, (o, d) in enumerate(eight):
        go(gb.at[piece(h, y)], gb.at[piece(h, y)], kgb[i], ts[o], yn[d])
    prep_s(2, 1, 0)
    unit_q(0, 0)
    first(4, 0)
    first(5, 0)
    prep_s(3, 1, 1)
    unit_p(0, 1)
    first(0, 1)
    first(1, 1)
    for i, (o, d) in enumerate(eight):
        arrived(gb.at[piece(hs[o], (y + 4 - d) % NY)], kgb[i])
    gw[...] = gb[...]
    eye(li)
    prep_s(1, 0, 1)
    factor(gw, li, FAC[0])
    unit_q(0, 1)
    first(4, 1)
    first(5, 1)
    second(0)
    second(1)
    factor(gw, li, FAC[1])
    unit_p(1, 0)
    first(2, 0)
    first(3, 0)
    second(4)
    second(5)
    factor(gw, li, FAC[2])
    unit_q(1, 0)
    first(6, 0)
    first(7, 0)
    factor(gw, li, FAC[3])
    unit_p(1, 1)
    first(2, 1)
    first(3, 1)
    last(0, p1.at[0])
    part(0, 0, p1.at[0])
    last(1, p1.at[1])
    part(0, 1, p1.at[1])
    factor(gw, li, FAC[4])
    unit_q(1, 1)
    first(6, 1)
    first(7, 1)
    second(2)
    second(3)
    last(4, q1.at[0])
    part(1, 0, q1.at[0])
    last(5, q1.at[1])
    part(1, 1, q1.at[1])
    second(6)
    second(7)
    factor(gw, li, FAC[5])
    root = float(NX * NZ * PR) ** 0.5
    own_s = s_ext[pl.ds(pl.multiple_of(16 + R * h, 16), R), :]
    basis_o[...] = lax.dot_general(own_s, li[...], NT_DOT, precision=HI, preferred_element_type=F32) * root
    last(2, p1.at[2])
    part(0, 2, p1.at[2])
    last(6, q1.at[2])
    part(1, 2, q1.at[2])
    last(3, p1.at[3])
    last(7, q1.at[3])
    part(0, 3, p1.at[3], raw.at[0])
    part(1, 3, q1.at[3], raw.at[1])
    for j in range(2):
        coef_o[j] = lax.dot_general(raw[j], li[...], NT_DOT, precision=HI, preferred_element_type=F32)

    for c in outs:
        c.wait_send()
    heads[0].wait_send()
    heads[1].wait_send()

    @pl.when(gives)
    def _():
        halos[0].wait_send()
        halos[1].wait_send()


FAC = (range(0, 3), range(3, 6), range(6, 9), range(9, 12), range(12, 16), range(16, 16))


def eye(li):
    rows = lax.broadcasted_iota(jnp.int32, (K, K), 0)
    cols = lax.broadcasted_iota(jnp.int32, (K, K), 1)
    li[...] = jnp.where(rows == cols, 1.0, 0.0).astype(F32)


def factor(g, li, blocks):
    for jb in blocks:
        base = 8 * jb
        rows = lax.broadcasted_iota(jnp.int32, (K - base, 1), 0)
        av, bv = g[base:], li[base:]
        for j in range(8):
            at_j = slice(base + j, base + j + 1)
            r = lax.rsqrt(av[j : j + 1, at_j])
            ra, rb = av[j : j + 1] * r, bv[j : j + 1] * r
            f = jnp.where(rows > j, av[:, at_j] * r, 0.0)
            av = av - f * ra
            bv = jnp.where(rows == j, rb, bv - f * rb)
        g[base:] = av
        li[base:] = bv


N_SEM = 4 + 3 + 3 + 4 + 48 + 12 + 7 + 3 + 3 + 7


def on_device(record, test_matrix):
    V = pl.BlockSpec(memory_space=pltpu.VMEM)
    H = pl.BlockSpec(memory_space=pl.ANY)
    return pl.pallas_call(
        body,
        out_shape=(jax.ShapeDtypeStruct((R, K), F32), jax.ShapeDtypeStruct((2, CH, K), F32)),
        in_specs=[H, H],
        out_specs=(V, V),
        scratch_shapes=[
            pltpu.VMEM((PR + 64, CH), F32),
            pltpu.VMEM((8, A, 2, CH, K), F32),
            pltpu.VMEM((R + 16, KC), BF16),
            pltpu.VMEM((2, KC, 2 * K), BF16),
            pltpu.VMEM((2, R // 2 + 16, K), F32),
            pltpu.VMEM((R, K), F32),
            pltpu.VMEM((3, 256, K), F32),
            pltpu.VMEM((PR + 32, K), F32),
            pltpu.VMEM((A * CH, KT), BF16),
            pltpu.VMEM((4, KT, 2 * K), BF16),
            pltpu.VMEM((8, A * CH, K), F32),
            pltpu.VMEM((8, 6, 128, K), F32),
            pltpu.VMEM((4, CH, K), F32),
            pltpu.VMEM((4, CH, K), F32),
            pltpu.VMEM((6, 128, K), F32),
            pltpu.VMEM((6, 128, K), F32),
            pltpu.VMEM((2, CH, K), F32),
            pltpu.VMEM((K, K), F32),
            pltpu.VMEM((7, 16, K), F32),
            pltpu.VMEM((3, 16, K), F32),
            pltpu.VMEM((4, 16, K), F32),
            pltpu.VMEM((K, K), F32),
            pltpu.VMEM((K, K), F32),
            pltpu.VMEM((K, K), F32),
            pltpu.SemaphoreType.DMA((33,)),
            pltpu.SemaphoreType.DMA((N_SEM,)),
            pltpu.SemaphoreType.DMA((N_SEM,)),
        ],
        compiler_params=pltpu.CompilerParams(collective_id=0, has_side_effects=True, vmem_limit_bytes=60 * 2**20),
    )(record, test_matrix)


def solution(mesh):
    return jax.shard_map(
        on_device,
        mesh=mesh,
        in_specs=(P("tm", "chan"), P(None, "chan", None)),
        out_specs=(P("tm", None), P("tm", "chan", None)),
        check_vma=False,
    )
```

```python
import jax
import jax.numpy as jnp
from jax import lax
from jax.experimental import pallas as pl
from jax.experimental.pallas import tpu as pltpu
from jax.sharding import PartitionSpec as P

F32, BF16 = jnp.float32, jnp.bfloat16
MESH = pl.DeviceIdType.MESH
NX, NZ, NY = 4, 4, 4
LAGS, CH, K = 64, 256, 128
R = 1024
PR = 2 * R
A = 4
KC = 3 * A * CH
KT = 3 * PR + 128
NT_DOT = (((1,), (1,)), ((), ()))
TN_DOT = (((0,), (0,)), ((), ()))
HI = lax.Precision.HIGHEST


def halves(v):
    hi = v.astype(BF16)
    return hi, (v - hi.astype(F32)).astype(BF16)


def body(rec, w, basis_o, coef_o, xe, wf, xcat, rhs, yb, acc, ry, s_ext, xt, srhs, cp,
         xr, p1, q1, pz, qz, raw, gm, ge, gx, gz, gb, gw, li, lsem, ss, rs):
    tm = lax.axis_index("tm")
    y = lax.axis_index("chan")
    h = tm % 2
    chip = tm // 2
    z = chip % NZ
    x = chip // NZ

    def at(xx, zz, hh):
        return (xx * NZ + zz) * 2 + hh

    sib = at(x, z, 1 - h)
    xn = [at((x + d) % NX, z, h) for d in range(NX)]
    zn = [at(x, (z + d) % NZ, h) for d in range(NZ)]
    yn = [(y + d) % NY for d in range(NY)]

    def send(src, dst, k, dt, dy):
        return pltpu.make_async_remote_copy(src_ref=src, dst_ref=dst, send_sem=ss.at[k], recv_sem=rs.at[k],
                                            device_id=(dt, dy), device_id_type=MESH)

    def arrived(ref, k):
        send(ref, ref, k, sib, y).wait_recv()

    count = [0]

    def sem():
        count[0] += 1
        return count[0] - 1

    own0 = pl.multiple_of(R * h, R)
    lx = pltpu.make_async_copy(rec, xe.at[pl.ds(own0, R)], lsem.at[0])
    lx.start()
    wcopies = []
    for p in range(8):
        for a in range(A):
            c = pltpu.make_async_copy(w.at[pl.ds(16 * a + 2 * p, 2)], wf.at[p, a], lsem.at[1 + 4 * p + a])
            c.start()
            wcopies.append(c)

    bar = pltpu.get_barrier_semaphore()

    def greet(dt, dy):
        pl.semaphore_signal(bar, inc=1, device_id=(dt, dy), device_id_type=MESH)

    greet(sib, y)
    for d in range(1, 4):
        greet(tm, yn[d])
        greet(sib, yn[d])
        greet(xn[d], y)
        greet(zn[d], y)
    gives = jnp.logical_and(h == 0, chip > 0)
    takes = chip < NX * NZ - 1
    down0, down1 = lax.max(tm - 2, 0), lax.max(tm - 1, 0)
    up = lax.min(2 * chip + 2, 2 * NX * NZ - 2)

    @pl.when(gives)
    def _():
        greet(down0, y)
        greet(down1, y)

    @pl.when(takes)
    def _():
        greet(up, y)

    def prep_w(p, slot):
        for a in range(A):
            for j in range(2):
                hi, lo = halves(wf[p, a, j])
                cs = pl.ds(128 * j, 128)
                rhs[slot, pl.ds(a * CH, CH), cs] = hi
                rhs[slot, pl.ds((A + a) * CH, CH), cs] = lo
                rhs[slot, pl.ds((2 * A + a) * CH, CH), cs] = hi

    def prep_x(i):
        for a in range(A):
            hi, lo = halves(xe[pl.ds(pl.multiple_of(R * h + 80 * i + 16 * a, 16), 80), :])
            rows = pl.ds(pl.multiple_of(80 * i, 16), 80)
            xcat[rows, pl.ds(a * CH, CH)] = hi
            xcat[rows, pl.ds((A + a) * CH, CH)] = hi
            xcat[rows, pl.ds((2 * A + a) * CH, CH)] = lo

    acc[...] = jnp.zeros_like(acc)
    zpad = jnp.zeros((16, K), F32)
    s_ext[pl.ds(0, 16)] = zpad
    s_ext[pl.ds(16 + PR, 16)] = zpad
    lx.wait()
    pl.loop(0, 12)(prep_x)
    for c in wcopies[:4]:
        c.wait()
    prep_w(0, 0)
    pl.semaphore_wait(bar, 13 + jnp.where(gives, 2, 0) + jnp.where(takes, 1, 0))

    kh0, kh1, ks0, ks1 = sem(), sem(), sem(), sem()
    halo = xe.at[pl.ds(PR, 64)]
    heads = [send(rec.at[pl.ds(0, 64)], xe.at[pl.ds(own0, 64)], ks0, sib, y),
             send(rec.at[pl.ds(64, R - 64)], xe.at[pl.ds(pl.multiple_of(own0 + 64, 64), R - 64)], ks1, sib, y)]
    halos = [pltpu.make_async_remote_copy(src_ref=rec.at[pl.ds(0, 64)], dst_ref=halo, send_sem=ss.at[kk],
                                          recv_sem=rs.at[kh0], device_id=(dd, y), device_id_type=MESH)
             for kk, dd in ((kh0, down0), (kh1, down1))]

    @pl.when(gives)
    def _():
        halos[0].start()
        halos[1].start()

    heads[0].start()
    heads[1].start()
    for c in wcopies[4:]:
        c.wait()
    oth0 = pl.multiple_of(R - R * h, R)
    outs = []

    def go(src, dst, k, dt, dy=y):
        c = send(src, dst, k, dt, dy)
        c.start()
        outs.append(c)

    kry = [sem() for _ in range(3)]
    ycopies = {d: send(acc.at[pl.ds(pl.multiple_of(yn[d] * 256, 256), 256)], ry.at[d - 1], kry[d - 1], tm, yn[d])
               for d in (2, 1, 3)}
    HR = R // 2
    for half in range(2):
        if half == 1:
            @pl.when(jnp.logical_not(takes))
            def _():
                halo[...] = jnp.zeros((64, CH), F32)

            @pl.when(takes)
            def _():
                arrived(halo, kh0)

            arrived(xe.at[pl.ds(oth0, 64)], ks0)
            prep_x(12)

        @pl.loop(0, 8)
        def _(p):
            slot = p % 2
            res = jnp.dot(xcat[pl.ds(HR * half, HR + 16)], rhs[slot], preferred_element_type=F32)
            yb[0] = res[:, :K]
            yb[1] = res[:, K:]
            prep_w((p + 1) % 8, 1 - slot)
            acc[pl.ds(HR * half, HR)] += yb[0, pl.ds(2 * p, HR), :] + yb[1, pl.ds(2 * p + 1, HR), :]

        for d in (2, 1, 3):
            pl.when(yn[d] // 2 == half)(ycopies[d].start)
    outs.extend(ycopies.values())
    arrived(xe.at[pl.ds(pl.multiple_of(oth0 + 64, 64), R - 64)], ks1)

    order = (2, 1, 3, 0)
    shift = [16 * ((x + o) % 4) for o in order]

    def xprep(i):
        cols = pl.multiple_of(128 * i, 128)
        for a in range(A):
            v = xe[pl.ds(pl.multiple_of(128 * i + shift[a], 16), 128), :].T
            hi, lo = halves(v)
            rows = pl.ds(a * CH, CH)
            xt[rows, pl.ds(cols, 128)] = hi
            xt[rows, pl.ds(pl.multiple_of(PR + cols, 128), 128)] = hi
            xt[rows, pl.ds(pl.multiple_of(2 * PR + cols, 128), 128)] = lo

    for a in range(A):
        v = xe[pl.ds(pl.multiple_of(PR + shift[a], 16), 16), :]
        hi = v.astype(BF16).astype(F32)
        t = jnp.concatenate([hi, hi, v - hi, jnp.zeros((80, CH), F32)], axis=0)
        xt[pl.ds(a * CH, CH), pl.ds(3 * PR, 128)] = t.T.astype(BF16)
    pl.loop(0, 8)(xprep)
    for d in range(1, 4):
        arrived(ry.at[d - 1], kry[d - 1])
    own_q = pl.ds(pl.multiple_of(y * 256, 256), 256)
    mine = pl.ds(pl.multiple_of(16 + R * h + 256 * y, 16), 256)
    s_ext[mine] = (acc[own_q] + ry[0]) + (ry[1] + ry[2])

    kag = [sem() for _ in range(3)]
    kfw = [sem() for _ in range(4)]
    kge = [sem() for _ in range(7)]
    kgx = [sem() for _ in range(3)]
    kgz = [sem() for _ in range(3)]
    kgb = [sem() for _ in range(7)]

    def place(hh, yy):
        return s_ext.at[pl.ds(pl.multiple_of(16 + R * hh + 256 * yy, 16), 256)]

    def piece(hh, yy):
        return pl.ds(pl.multiple_of((hh * NY + yy) * 16, 16), 16)

    sv = s_ext[mine]
    gm[...] = lax.dot_general(sv, sv, TN_DOT, precision=HI, preferred_element_type=F32)
    eight = [(0, 1), (0, 2), (0, 3), (1, 0), (1, 1), (1, 2), (1, 3)]
    hs, ts = (h, 1 - h), (tm, sib)
    for i, (o, d) in enumerate(eight):
        go(gm.at[piece(hs[o], yn[d])], ge.at[i], kge[i], ts[o], yn[d])
    go(place(h, y), place(h, y), kfw[0], sib)
    for d in (2, 1, 3):
        go(place(h, y), place(h, y), kag[d - 1], tm, yn[d])
    pl.loop(8, 16)(xprep)
    for i in range(7):
        arrived(ge.at[i], kge[i])
    gm[piece(h, y)] = (((gm[piece(h, y)] + ge[0]) + (ge[1] + ge[2])) + ((ge[3] + ge[4]) + (ge[5] + ge[6])))
    for d in range(1, 4):
        go(gm.at[piece(h, y)], gx.at[d - 1], kgx[d - 1], xn[d])

    def forward(d):
        src = place(h, (y + 4 - d) % NY)
        arrived(src, kag[d - 1])
        go(src, src, kfw[d], sib)

    forward(1)
    forward(3)
    forward(2)
    for d in range(1, 4):
        arrived(gx.at[d - 1], kgx[d - 1])
    gz[3] = (gm[piece(h, y)] + gx[0]) + (gx[1] + gx[2])
    for d in range(1, 4):
        go(gz.at[3], gz.at[d - 1], kgz[d - 1], zn[d])
    for d in range(4):
        arrived(place(1 - h, (y + 4 - d) % NY), kfw[d])

    def prep_s(n, j, pair):
        for c in range(2):
            cs = pl.ds(128 * c, 128)
            off = 16 - j - 2 * h - 4 * ((z + order[2 * pair + c]) % NZ)
            hi, lo = halves(s_ext[pl.ds(off, PR), :])
            srhs[n, pl.ds(0, PR), cs] = hi
            srhs[n, pl.ds(PR, PR), cs] = lo
            srhs[n, pl.ds(2 * PR, PR), cs] = hi
            hi, lo = halves(s_ext[pl.ds(PR + off, 16), :])
            srhs[n, pl.ds(3 * PR, 16), cs] = hi
            srhs[n, pl.ds(3 * PR + 16, 16), cs] = lo
            srhs[n, pl.ds(3 * PR + 32, 16), cs] = hi
            srhs[n, pl.ds(3 * PR + 48, 80), cs] = jnp.zeros((80, K), BF16)

    def unit_p(t, u):
        rows = pl.ds(512 * u, 512)
        res = jnp.dot(xt[rows, :], srhs[t], preferred_element_type=F32)
        for c in range(2):
            cp[2 * t + c, rows, :] = res[:, 128 * c : 128 * c + 128]

    def unit_q(t, u):
        res = jnp.dot(xt[pl.ds(512 * t, 512), :], srhs[2 + u], preferred_element_type=F32)
        for m in range(2):
            for c in range(2):
                cp[4 + 2 * t + m, pl.ds(256 * (2 * u + c), 256), :] = res[256 * m : 256 * m + 256, 128 * c : 128 * c + 128]

    rk = [[sem() for _ in range(6)] for _ in range(8)]

    def ends(n):
        return (xn[1], xn[3]) if n < 4 else (zn[1], zn[3])

    def first(n, u):
        up, dn = ends(n)
        src, buf = cp.at[n], xr.at[n]
        if u == 0:
            go(src.at[0:128], buf.at[0], rk[n][0], up)
            go(src.at[128:256], buf.at[1], rk[n][1], dn)
            go(src.at[384:512], buf.at[3], rk[n][3], up)
        else:
            go(src.at[512:640], buf.at[2], rk[n][2], dn)

    def second(n):
        up, dn = ends(n)
        arrived(xr.at[n, 0], rk[n][0])
        cp[n, 256:384] += xr[n, 0]
        go(cp.at[n, 256:384], xr.at[n, 4], rk[n][4], up)
        arrived(xr.at[n, 1], rk[n][1])
        cp[n, 640:768] += xr[n, 1]
        go(cp.at[n, 640:768], xr.at[n, 5], rk[n][5], dn)

    def last(n, dst):
        for i in (2, 3, 4, 5):
            arrived(xr.at[n, i], rk[n][i])
        dst[0:128] = cp[n, 768:896] + (xr[n, 2] + xr[n, 4])
        dst[128:256] = cp[n, 896:1024] + (xr[n, 3] + xr[n, 5])

    zk = [[sem() for _ in range(6)] for _ in range(2)]

    def part_own(q, t, src):
        up, dn = ends(0 if q else 4)
        buf, ks = (pz, qz)[q], zk[q]
        a, b = src.at[0:128], src.at[128:256]
        if t == 0:
            go(a, buf.at[0], ks[0], up)
            go(b, buf.at[1], ks[1], dn)
        elif t == 1:
            go(b, buf.at[3], ks[3], up)
        else:
            go(a, buf.at[2], ks[2], dn)

    def part_on(q, t, src):
        up, dn = ends(0 if q else 4)
        buf, ks = (pz, qz)[q], zk[q]
        half, to = (pl.ds(0, 128), up) if t == 1 else (pl.ds(128, 128), dn)
        arrived(buf.at[t - 1], ks[t - 1])
        src[half] += buf[t - 1]
        go(src.at[half], buf.at[3 + t], ks[3 + t], to)

    def part_sum(q, src, dst):
        buf, ks = (pz, qz)[q], zk[q]
        for i in (2, 3, 4, 5):
            arrived(buf.at[i], ks[i])
        dst[0:128] = src[0:128] + (buf[2] + buf[4])
        dst[128:256] = src[128:256] + (buf[3] + buf[5])

    def p_last(n):
        last(n, p1.at[n])
        part_own(0, n, p1.at[n])

    def q_last(n):
        last(4 + n, q1.at[n])
        part_own(1, n, q1.at[n])

    prep_s(0, 0, 0)
    unit_p(0, 0)
    first(0, 0)
    first(1, 0)
    for d in range(1, 4):
        arrived(gz.at[d - 1], kgz[d - 1])
    gb[piece(h, y)] = (gz[3] + gz[0]) + (gz[1] + gz[2])
    for i, (o, d) in enumerate(eight):
        go(gb.at[piece(h, y)], gb.at[piece(h, y)], kgb[i], ts[o], yn[d])
    prep_s(2, 1, 0)
    unit_q(0, 0)
    first(4, 0)
    first(5, 0)
    prep_s(3, 1, 1)
    unit_p(0, 1)
    first(0, 1)
    first(1, 1)
    for i, (o, d) in enumerate(eight):
        arrived(gb.at[piece(hs[o], (y + 4 - d) % NY)], kgb[i])
    gw[...] = gb[...]
    eye(li)
    prep_s(1, 0, 1)
    factor(gw, li, FAC[0])
    unit_q(0, 1)
    first(4, 1)
    first(5, 1)
    second(0)
    second(1)
    factor(gw, li, FAC[1])
    unit_p(1, 0)
    first(2, 0)
    first(3, 0)
    second(4)
    second(5)
    factor(gw, li, FAC[2])
    unit_q(1, 0)
    first(6, 0)
    first(7, 0)
    p_last(0)
    p_last(1)
    factor(gw, li, FAC[3])
    unit_p(1, 1)
    first(2, 1)
    first(3, 1)
    second(2)
    second(3)
    q_last(0)
    q_last(1)
    factor(gw, li, FAC[4])
    unit_q(1, 1)
    first(6, 1)
    first(7, 1)
    second(6)
    second(7)
    part_on(0, 1, p1.at[1])
    part_on(1, 1, q1.at[1])
    root = float(NX * NZ * PR) ** 0.5
    own_s = s_ext[pl.ds(pl.multiple_of(16 + R * h, 16), R), :]
    basis_o[...] = lax.dot_general(own_s, li[...], NT_DOT, precision=HI, preferred_element_type=F32) * root
    p_last(2)
    part_on(0, 2, p1.at[2])
    q_last(2)
    part_on(1, 2, q1.at[2])
    last(3, p1.at[3])
    last(7, q1.at[3])
    part_sum(0, p1.at[3], raw.at[0])
    part_sum(1, q1.at[3], raw.at[1])
    for j in range(2):
        coef_o[j] = lax.dot_general(raw[j], li[...], NT_DOT, precision=HI, preferred_element_type=F32)

    for c in outs:
        c.wait_send()
    heads[0].wait_send()
    heads[1].wait_send()

    @pl.when(gives)
    def _():
        halos[0].wait_send()
        halos[1].wait_send()


FAC = (range(0, 3), range(3, 6), range(6, 9), range(9, 12), range(12, 16))


def eye(li):
    rows = lax.broadcasted_iota(jnp.int32, (K, K), 0)
    cols = lax.broadcasted_iota(jnp.int32, (K, K), 1)
    li[...] = jnp.where(rows == cols, 1.0, 0.0).astype(F32)


def factor(g, li, blocks):
    for jb in blocks:
        base = 8 * jb
        rows = lax.broadcasted_iota(jnp.int32, (K - base, 1), 0)
        av, bv = g[base:], li[base:]
        for j in range(8):
            at_j = slice(base + j, base + j + 1)
            r = lax.rsqrt(av[j : j + 1, at_j])
            ra, rb = av[j : j + 1] * r, bv[j : j + 1] * r
            f = jnp.where(rows > j, av[:, at_j] * r, 0.0)
            av = av - f * ra
            bv = jnp.where(rows == j, rb, bv - f * rb)
        g[base:] = av
        li[base:] = bv


N_SEM = 4 + 3 + 3 + 4 + 48 + 12 + 7 + 3 + 3 + 7


def on_device(record, test_matrix):
    V = pl.BlockSpec(memory_space=pltpu.VMEM)
    H = pl.BlockSpec(memory_space=pl.ANY)
    return pl.pallas_call(
        body,
        out_shape=(jax.ShapeDtypeStruct((R, K), F32), jax.ShapeDtypeStruct((2, CH, K), F32)),
        in_specs=[H, H],
        out_specs=(V, V),
        scratch_shapes=[
            pltpu.VMEM((PR + 64, CH), F32),
            pltpu.VMEM((8, A, 2, CH, K), F32),
            pltpu.VMEM((R + 16, KC), BF16),
            pltpu.VMEM((2, KC, 2 * K), BF16),
            pltpu.VMEM((2, R // 2 + 16, K), F32),
            pltpu.VMEM((R, K), F32),
            pltpu.VMEM((3, 256, K), F32),
            pltpu.VMEM((PR + 32, K), F32),
            pltpu.VMEM((A * CH, KT), BF16),
            pltpu.VMEM((4, KT, 2 * K), BF16),
            pltpu.VMEM((8, A * CH, K), F32),
            pltpu.VMEM((8, 6, 128, K), F32),
            pltpu.VMEM((4, CH, K), F32),
            pltpu.VMEM((4, CH, K), F32),
            pltpu.VMEM((6, 128, K), F32),
            pltpu.VMEM((6, 128, K), F32),
            pltpu.VMEM((2, CH, K), F32),
            pltpu.VMEM((K, K), F32),
            pltpu.VMEM((7, 16, K), F32),
            pltpu.VMEM((3, 16, K), F32),
            pltpu.VMEM((4, 16, K), F32),
            pltpu.VMEM((K, K), F32),
            pltpu.VMEM((K, K), F32),
            pltpu.VMEM((K, K), F32),
            pltpu.SemaphoreType.DMA((33,)),
            pltpu.SemaphoreType.DMA((N_SEM,)),
            pltpu.SemaphoreType.DMA((N_SEM,)),
        ],
        compiler_params=pltpu.CompilerParams(collective_id=0, has_side_effects=True, vmem_limit_bytes=60 * 2**20),
    )(record, test_matrix)


def solution(mesh):
    return jax.shard_map(
        on_device,
        mesh=mesh,
        in_specs=(P("tm", "chan"), P(None, "chan", None)),
        out_specs=(P("tm", None), P("tm", "chan", None)),
        check_vma=False,
    )
```

```python
import jax
import jax.numpy as jnp
from jax import lax
from jax.experimental import pallas as pl
from jax.experimental.pallas import tpu as pltpu
from jax.sharding import PartitionSpec as P

F32, BF16 = jnp.float32, jnp.bfloat16
MESH = pl.DeviceIdType.MESH
NX, NZ, NY = 4, 4, 4
LAGS, CH, K = 64, 256, 128
R = 1024
PR = 2 * R
A = 4
KC = 3 * A * CH
KT = 3 * PR + 128
NT_DOT = (((1,), (1,)), ((), ()))
TN_DOT = (((0,), (0,)), ((), ()))
HI = lax.Precision.HIGHEST


def halves(v):
    hi = v.astype(BF16)
    return hi, (v - hi.astype(F32)).astype(BF16)


def body(rec, w, s_o, raw, li_o, xe, wf, xcat, rhs, yb, acc, ry, s_ext, xt, srhs, cp,
         xr, p1, q1, pz, qz, gm, ge, gx, gz, gb, gw, li, lsem, ss, rs):
    tm = lax.axis_index("tm")
    y = lax.axis_index("chan")
    h = tm % 2
    chip = tm // 2
    z = chip % NZ
    x = chip // NZ

    def at(xx, zz, hh):
        return (xx * NZ + zz) * 2 + hh

    sib = at(x, z, 1 - h)
    xn = [at((x + d) % NX, z, h) for d in range(NX)]
    zn = [at(x, (z + d) % NZ, h) for d in range(NZ)]
    yn = [(y + d) % NY for d in range(NY)]

    def send(src, dst, k, dt, dy):
        return pltpu.make_async_remote_copy(src_ref=src, dst_ref=dst, send_sem=ss.at[k], recv_sem=rs.at[k],
                                            device_id=(dt, dy), device_id_type=MESH)

    def arrived(ref, k):
        send(ref, ref, k, sib, y).wait_recv()

    count = [0]

    def sem():
        count[0] += 1
        return count[0] - 1

    own0 = pl.multiple_of(R * h, R)
    lx = pltpu.make_async_copy(rec, xe.at[pl.ds(own0, R)], lsem.at[0])
    lx.start()
    wcopies = []
    for p in range(8):
        for a in range(A):
            c = pltpu.make_async_copy(w.at[pl.ds(16 * a + 2 * p, 2)], wf.at[p, a], lsem.at[1 + 4 * p + a])
            c.start()
            wcopies.append(c)

    bar = pltpu.get_barrier_semaphore()

    def greet(dt, dy):
        pl.semaphore_signal(bar, inc=1, device_id=(dt, dy), device_id_type=MESH)

    greet(sib, y)
    for d in range(1, 4):
        greet(tm, yn[d])
        greet(sib, yn[d])
        greet(xn[d], y)
        greet(zn[d], y)
    gives = jnp.logical_and(h == 0, chip > 0)
    takes = chip < NX * NZ - 1
    down0, down1 = lax.max(tm - 2, 0), lax.max(tm - 1, 0)
    up = lax.min(2 * chip + 2, 2 * NX * NZ - 2)

    @pl.when(gives)
    def _():
        greet(down0, y)
        greet(down1, y)

    @pl.when(takes)
    def _():
        greet(up, y)

    def prep_w(p, slot):
        for a in range(A):
            for j in range(2):
                hi, lo = halves(wf[p, a, j])
                cs = pl.ds(128 * j, 128)
                rhs[slot, pl.ds(a * CH, CH), cs] = hi
                rhs[slot, pl.ds((A + a) * CH, CH), cs] = lo
                rhs[slot, pl.ds((2 * A + a) * CH, CH), cs] = hi

    def prep_x(i):
        for a in range(A):
            hi, lo = halves(xe[pl.ds(pl.multiple_of(R * h + 80 * i + 16 * a, 16), 80), :])
            rows = pl.ds(pl.multiple_of(80 * i, 16), 80)
            xcat[rows, pl.ds(a * CH, CH)] = hi
            xcat[rows, pl.ds((A + a) * CH, CH)] = hi
            xcat[rows, pl.ds((2 * A + a) * CH, CH)] = lo

    acc[...] = jnp.zeros_like(acc)
    zpad = jnp.zeros((16, K), F32)
    s_ext[pl.ds(0, 16)] = zpad
    s_ext[pl.ds(16 + PR, 16)] = zpad
    lx.wait()
    pl.loop(0, 12)(prep_x)
    for c in wcopies[:4]:
        c.wait()
    prep_w(0, 0)
    pl.semaphore_wait(bar, 13 + jnp.where(gives, 2, 0) + jnp.where(takes, 1, 0))

    kh0, kh1, ks0, ks1 = sem(), sem(), sem(), sem()
    halo = xe.at[pl.ds(PR, 64)]
    heads = [send(rec.at[pl.ds(0, 64)], xe.at[pl.ds(own0, 64)], ks0, sib, y),
             send(rec.at[pl.ds(64, R - 64)], xe.at[pl.ds(pl.multiple_of(own0 + 64, 64), R - 64)], ks1, sib, y)]
    halos = [pltpu.make_async_remote_copy(src_ref=rec.at[pl.ds(0, 64)], dst_ref=halo, send_sem=ss.at[kk],
                                          recv_sem=rs.at[kh0], device_id=(dd, y), device_id_type=MESH)
             for kk, dd in ((kh0, down0), (kh1, down1))]

    @pl.when(gives)
    def _():
        halos[0].start()
        halos[1].start()

    heads[0].start()
    heads[1].start()
    for c in wcopies[4:]:
        c.wait()
    oth0 = pl.multiple_of(R - R * h, R)
    outs = []

    def go(src, dst, k, dt, dy=y):
        c = send(src, dst, k, dt, dy)
        c.start()
        outs.append(c)

    kry = [sem() for _ in range(3)]
    ycopies = {d: send(acc.at[pl.ds(pl.multiple_of(yn[d] * 256, 256), 256)], ry.at[d - 1], kry[d - 1], tm, yn[d])
               for d in (2, 1, 3)}
    HR = R // 2
    for half in range(2):
        if half == 1:
            @pl.when(jnp.logical_not(takes))
            def _():
                halo[...] = jnp.zeros((64, CH), F32)

            @pl.when(takes)
            def _():
                arrived(halo, kh0)

            arrived(xe.at[pl.ds(oth0, 64)], ks0)
            prep_x(12)

        @pl.loop(0, 8)
        def _(p):
            slot = p % 2
            res = jnp.dot(xcat[pl.ds(HR * half, HR + 16)], rhs[slot], preferred_element_type=F32)
            yb[0] = res[:, :K]
            yb[1] = res[:, K:]
            prep_w((p + 1) % 8, 1 - slot)
            acc[pl.ds(HR * half, HR)] += yb[0, pl.ds(2 * p, HR), :] + yb[1, pl.ds(2 * p + 1, HR), :]

        for d in (2, 1, 3):
            pl.when(yn[d] // 2 == half)(ycopies[d].start)
    outs.extend(ycopies.values())
    arrived(xe.at[pl.ds(pl.multiple_of(oth0 + 64, 64), R - 64)], ks1)

    order = (2, 1, 3, 0)
    shift = [16 * ((x + o) % 4) for o in order]

    def xprep(i):
        cols = pl.multiple_of(128 * i, 128)
        for a in range(A):
            v = xe[pl.ds(pl.multiple_of(128 * i + shift[a], 16), 128), :].T
            hi, lo = halves(v)
            rows = pl.ds(a * CH, CH)
            xt[rows, pl.ds(cols, 128)] = hi
            xt[rows, pl.ds(pl.multiple_of(PR + cols, 128), 128)] = hi
            xt[rows, pl.ds(pl.multiple_of(2 * PR + cols, 128), 128)] = lo

    for a in range(A):
        v = xe[pl.ds(pl.multiple_of(PR + shift[a], 16), 16), :]
        hi = v.astype(BF16).astype(F32)
        t = jnp.concatenate([hi, hi, v - hi, jnp.zeros((80, CH), F32)], axis=0)
        xt[pl.ds(a * CH, CH), pl.ds(3 * PR, 128)] = t.T.astype(BF16)
    pl.loop(0, 8)(xprep)
    for d in range(1, 4):
        arrived(ry.at[d - 1], kry[d - 1])
    own_q = pl.ds(pl.multiple_of(y * 256, 256), 256)
    mine = pl.ds(pl.multiple_of(16 + R * h + 256 * y, 16), 256)
    s_ext[mine] = (acc[own_q] + ry[0]) + (ry[1] + ry[2])

    kag = [sem() for _ in range(3)]
    kfw = [sem() for _ in range(4)]
    kge = [sem() for _ in range(7)]
    kgx = [sem() for _ in range(3)]
    kgz = [sem() for _ in range(3)]
    kgb = [sem() for _ in range(7)]

    def place(hh, yy):
        return s_ext.at[pl.ds(pl.multiple_of(16 + R * hh + 256 * yy, 16), 256)]

    def piece(hh, yy):
        return pl.ds(pl.multiple_of((hh * NY + yy) * 16, 16), 16)

    sv = s_ext[mine]
    gm[...] = lax.dot_general(sv, sv, TN_DOT, precision=HI, preferred_element_type=F32)
    eight = [(0, 1), (0, 2), (0, 3), (1, 0), (1, 1), (1, 2), (1, 3)]
    hs, ts = (h, 1 - h), (tm, sib)
    for i, (o, d) in enumerate(eight):
        go(gm.at[piece(hs[o], yn[d])], ge.at[i], kge[i], ts[o], yn[d])
    go(place(h, y), place(h, y), kfw[0], sib)
    for d in (2, 1, 3):
        go(place(h, y), place(h, y), kag[d - 1], tm, yn[d])
    pl.loop(8, 16)(xprep)
    def forward(d):
        src = place(h, (y + 4 - d) % NY)
        arrived(src, kag[d - 1])
        go(src, src, kfw[d], sib)

    forward(1)
    forward(3)
    forward(2)
    for i in range(7):
        arrived(ge.at[i], kge[i])
    gm[piece(h, y)] = (((gm[piece(h, y)] + ge[0]) + (ge[1] + ge[2])) + ((ge[3] + ge[4]) + (ge[5] + ge[6])))
    for d in range(1, 4):
        go(gm.at[piece(h, y)], gx.at[d - 1], kgx[d - 1], xn[d])
    for d in range(4):
        arrived(place(1 - h, (y + 4 - d) % NY), kfw[d])

    def prep_s(n, j, pair):
        for c in range(2):
            cs = pl.ds(128 * c, 128)
            off = 16 - j - 2 * h - 4 * ((z + order[2 * pair + c]) % NZ)
            hi, lo = halves(s_ext[pl.ds(off, PR), :])
            srhs[n, pl.ds(0, PR), cs] = hi
            srhs[n, pl.ds(PR, PR), cs] = lo
            srhs[n, pl.ds(2 * PR, PR), cs] = hi
            hi, lo = halves(s_ext[pl.ds(PR + off, 16), :])
            srhs[n, pl.ds(3 * PR, 16), cs] = hi
            srhs[n, pl.ds(3 * PR + 16, 16), cs] = lo
            srhs[n, pl.ds(3 * PR + 32, 16), cs] = hi
            srhs[n, pl.ds(3 * PR + 48, 80), cs] = jnp.zeros((80, K), BF16)

    def unit_p(t, u):
        rows = pl.ds(512 * u, 512)
        res = jnp.dot(xt[rows, :], srhs[t], preferred_element_type=F32)
        for c in range(2):
            cp[2 * t + c, rows, :] = res[:, 128 * c : 128 * c + 128]

    def unit_q(t, u):
        res = jnp.dot(xt[pl.ds(512 * t, 512), :], srhs[2 + u], preferred_element_type=F32)
        for m in range(2):
            for c in range(2):
                cp[4 + 2 * t + m, pl.ds(256 * (2 * u + c), 256), :] = res[256 * m : 256 * m + 256, 128 * c : 128 * c + 128]

    rk = [[sem() for _ in range(6)] for _ in range(8)]

    def ends(n):
        return (xn[1], xn[3]) if n < 4 else (zn[1], zn[3])

    def first(n, u):
        up, dn = ends(n)
        src, buf = cp.at[n], xr.at[n]
        if u == 0:
            go(src.at[0:128], buf.at[0], rk[n][0], up)
            go(src.at[128:256], buf.at[1], rk[n][1], dn)
            go(src.at[384:512], buf.at[3], rk[n][3], up)
        else:
            go(src.at[512:640], buf.at[2], rk[n][2], dn)

    def second(n):
        up, dn = ends(n)
        arrived(xr.at[n, 0], rk[n][0])
        cp[n, 256:384] += xr[n, 0]
        go(cp.at[n, 256:384], xr.at[n, 4], rk[n][4], up)
        arrived(xr.at[n, 1], rk[n][1])
        cp[n, 640:768] += xr[n, 1]
        go(cp.at[n, 640:768], xr.at[n, 5], rk[n][5], dn)

    def last(n, dst):
        for i in (2, 3, 4, 5):
            arrived(xr.at[n, i], rk[n][i])
        dst[0:128] = cp[n, 768:896] + (xr[n, 2] + xr[n, 4])
        dst[128:256] = cp[n, 896:1024] + (xr[n, 3] + xr[n, 5])

    zk = [[sem() for _ in range(6)] for _ in range(2)]

    def part_own(q, t, src):
        up, dn = ends(0 if q else 4)
        buf, ks = (pz, qz)[q], zk[q]
        a, b = src.at[0:128], src.at[128:256]
        if t == 0:
            go(a, buf.at[0], ks[0], up)
            go(b, buf.at[1], ks[1], dn)
        elif t == 1:
            go(b, buf.at[3], ks[3], up)
        else:
            go(a, buf.at[2], ks[2], dn)

    def part_on(q, t, src):
        up, dn = ends(0 if q else 4)
        buf, ks = (pz, qz)[q], zk[q]
        half, to = (pl.ds(0, 128), up) if t == 1 else (pl.ds(128, 128), dn)
        arrived(buf.at[t - 1], ks[t - 1])
        src[half] += buf[t - 1]
        go(src.at[half], buf.at[3 + t], ks[3 + t], to)

    def part_sum(q, src, dst):
        buf, ks = (pz, qz)[q], zk[q]
        for i in (2, 3, 4, 5):
            arrived(buf.at[i], ks[i])
        dst[0:128] = src[0:128] + (buf[2] + buf[4])
        dst[128:256] = src[128:256] + (buf[3] + buf[5])

    def p_last(n):
        last(n, p1.at[n])
        part_own(0, n, p1.at[n])

    def q_last(n):
        last(4 + n, q1.at[n])
        part_own(1, n, q1.at[n])

    prep_s(0, 0, 0)
    unit_p(0, 0)
    first(0, 0)
    first(1, 0)
    for d in range(1, 4):
        arrived(gx.at[d - 1], kgx[d - 1])
    gz[3] = (gm[piece(h, y)] + gx[0]) + (gx[1] + gx[2])
    for d in range(1, 4):
        go(gz.at[3], gz.at[d - 1], kgz[d - 1], zn[d])
    prep_s(2, 1, 0)
    unit_q(0, 0)
    first(4, 0)
    first(5, 0)
    for d in range(1, 4):
        arrived(gz.at[d - 1], kgz[d - 1])
    gb[piece(h, y)] = (gz[3] + gz[0]) + (gz[1] + gz[2])
    for i, (o, d) in enumerate(eight):
        go(gb.at[piece(h, y)], gb.at[piece(h, y)], kgb[i], ts[o], yn[d])
    prep_s(3, 1, 1)
    unit_p(0, 1)
    first(0, 1)
    first(1, 1)
    for i, (o, d) in enumerate(eight):
        arrived(gb.at[piece(hs[o], (y + 4 - d) % NY)], kgb[i])
    gw[...] = gb[...]
    eye(li)
    prep_s(1, 0, 1)
    factor(gw, li, FAC[0])
    unit_q(0, 1)
    first(4, 1)
    first(5, 1)
    second(0)
    second(1)
    factor(gw, li, FAC[1])
    unit_p(1, 0)
    first(2, 0)
    first(3, 0)
    second(4)
    second(5)
    factor(gw, li, FAC[2])
    unit_q(1, 0)
    first(6, 0)
    first(7, 0)
    p_last(0)
    p_last(1)
    factor(gw, li, FAC[3])
    unit_p(1, 1)
    first(2, 1)
    first(3, 1)
    second(2)
    second(3)
    q_last(0)
    q_last(1)
    factor(gw, li, FAC[4])
    unit_q(1, 1)
    first(6, 1)
    first(7, 1)
    second(6)
    second(7)
    part_on(0, 1, p1.at[1])
    part_on(1, 1, q1.at[1])
    s_o[...] = s_ext[pl.ds(pl.multiple_of(16 + R * h, 16), R), :]
    li_o[...] = li[...]
    p_last(2)
    part_on(0, 2, p1.at[2])
    q_last(2)
    part_on(1, 2, q1.at[2])
    last(3, p1.at[3])
    last(7, q1.at[3])
    part_sum(0, p1.at[3], raw.at[0])
    part_sum(1, q1.at[3], raw.at[1])

    for c in outs:
        c.wait_send()
    heads[0].wait_send()
    heads[1].wait_send()

    @pl.when(gives)
    def _():
        halos[0].wait_send()
        halos[1].wait_send()


FAC = (range(0, 3), range(3, 6), range(6, 9), range(9, 12), range(12, 16))


def apply_inverse(own, raw, inv, basis, coeffs):
    root = float(NX * NZ * PR) ** 0.5
    basis[...] = lax.dot_general(own[...], inv[...], NT_DOT, precision=HI, preferred_element_type=F32) * root
    for j in range(2):
        coeffs[j] = lax.dot_general(raw[j], inv[...], NT_DOT, precision=HI, preferred_element_type=F32)


def eye(li):
    rows = lax.broadcasted_iota(jnp.int32, (K, K), 0)
    cols = lax.broadcasted_iota(jnp.int32, (K, K), 1)
    li[...] = jnp.where(rows == cols, 1.0, 0.0).astype(F32)


def factor(g, li, blocks):
    for jb in blocks:
        base = 8 * jb
        rows = lax.broadcasted_iota(jnp.int32, (K - base, 1), 0)
        av, bv = g[base:], li[base:]
        for j in range(8):
            at_j = slice(base + j, base + j + 1)
            r = lax.rsqrt(av[j : j + 1, at_j])
            ra, rb = av[j : j + 1] * r, bv[j : j + 1] * r
            f = jnp.where(rows > j, av[:, at_j] * r, 0.0)
            av = av - f * ra
            bv = jnp.where(rows == j, rb, bv - f * rb)
        g[base:] = av
        li[base:] = bv


N_SEM = 4 + 3 + 3 + 4 + 48 + 12 + 7 + 3 + 3 + 7


def on_device(record, test_matrix):
    V = pl.BlockSpec(memory_space=pltpu.VMEM)
    H = pl.BlockSpec(memory_space=pl.ANY)
    own, raw, inv = pl.pallas_call(
        body,
        out_shape=(
            jax.ShapeDtypeStruct((R, K), F32),
            jax.ShapeDtypeStruct((2, CH, K), F32),
            jax.ShapeDtypeStruct((K, K), F32),
        ),
        in_specs=[H, H],
        out_specs=(V, V, V),
        scratch_shapes=[
            pltpu.VMEM((PR + 64, CH), F32),
            pltpu.VMEM((8, A, 2, CH, K), F32),
            pltpu.VMEM((R + 16, KC), BF16),
            pltpu.VMEM((2, KC, 2 * K), BF16),
            pltpu.VMEM((2, R // 2 + 16, K), F32),
            pltpu.VMEM((R, K), F32),
            pltpu.VMEM((3, 256, K), F32),
            pltpu.VMEM((PR + 32, K), F32),
            pltpu.VMEM((A * CH, KT), BF16),
            pltpu.VMEM((4, KT, 2 * K), BF16),
            pltpu.VMEM((8, A * CH, K), F32),
            pltpu.VMEM((8, 6, 128, K), F32),
            pltpu.VMEM((4, CH, K), F32),
            pltpu.VMEM((4, CH, K), F32),
            pltpu.VMEM((6, 128, K), F32),
            pltpu.VMEM((6, 128, K), F32),
            pltpu.VMEM((K, K), F32),
            pltpu.VMEM((7, 16, K), F32),
            pltpu.VMEM((3, 16, K), F32),
            pltpu.VMEM((4, 16, K), F32),
            pltpu.VMEM((K, K), F32),
            pltpu.VMEM((K, K), F32),
            pltpu.VMEM((K, K), F32),
            pltpu.SemaphoreType.DMA((33,)),
            pltpu.SemaphoreType.DMA((N_SEM,)),
            pltpu.SemaphoreType.DMA((N_SEM,)),
        ],
        compiler_params=pltpu.CompilerParams(collective_id=0, has_side_effects=True, vmem_limit_bytes=60 * 2**20),
    )(record, test_matrix)
    return pl.pallas_call(
        apply_inverse,
        out_shape=(jax.ShapeDtypeStruct((R, K), F32), jax.ShapeDtypeStruct((2, CH, K), F32)),
        in_specs=[V, V, V],
        out_specs=(V, V),
    )(own, raw, inv)


def solution(mesh):
    return jax.shard_map(
        on_device,
        mesh=mesh,
        in_specs=(P("tm", "chan"), P(None, "chan", None)),
        out_specs=(P("tm", None), P("tm", "chan", None)),
        check_vma=False,
    )
```

```python
import jax
import jax.numpy as jnp
from jax import lax
from jax.experimental import pallas as pl
from jax.experimental.pallas import tpu as pltpu
from jax.sharding import PartitionSpec as P

F32, BF16 = jnp.float32, jnp.bfloat16
MESH = pl.DeviceIdType.MESH
NX, NZ, NY = 4, 4, 4
LAGS, CH, K = 64, 256, 128
R = 1024
PR = 2 * R
A = 4
KC = 3 * A * CH
KT = 3 * PR + 128
NT_DOT = (((1,), (1,)), ((), ()))
TN_DOT = (((0,), (0,)), ((), ()))
HI = lax.Precision.HIGHEST


def halves(v):
    hi = v.astype(BF16)
    return hi, (v - hi.astype(F32)).astype(BF16)


def body(rec, w, s_o, raw, li_o, xe, wf, xcat, rhs, yb, acc, ry, s_ext, xt, srhs, cp,
         xr, p1, q1, pz, qz, gm, ge, gx, gz, gb, gw, li, lsem, ss, rs):
    tm = lax.axis_index("tm")
    y = lax.axis_index("chan")
    h = tm % 2
    chip = tm // 2
    z = chip % NZ
    x = chip // NZ

    def at(xx, zz, hh):
        return (xx * NZ + zz) * 2 + hh

    sib = at(x, z, 1 - h)
    xn = [at((x + d) % NX, z, h) for d in range(NX)]
    zn = [at(x, (z + d) % NZ, h) for d in range(NZ)]
    yn = [(y + d) % NY for d in range(NY)]

    def send(src, dst, k, dt, dy):
        return pltpu.make_async_remote_copy(src_ref=src, dst_ref=dst, send_sem=ss.at[k], recv_sem=rs.at[k],
                                            device_id=(dt, dy), device_id_type=MESH)

    def arrived(ref, k):
        send(ref, ref, k, sib, y).wait_recv()

    count = [0]

    def sem():
        count[0] += 1
        return count[0] - 1

    own0 = pl.multiple_of(R * h, R)
    lx = pltpu.make_async_copy(rec, xe.at[pl.ds(own0, R)], lsem.at[0])
    lx.start()
    wcopies = []
    for p in range(8):
        for a in range(A):
            c = pltpu.make_async_copy(w.at[pl.ds(16 * a + 2 * p, 2)], wf.at[p, a], lsem.at[1 + 4 * p + a])
            c.start()
            wcopies.append(c)

    bar = pltpu.get_barrier_semaphore()

    def greet(dt, dy):
        pl.semaphore_signal(bar, inc=1, device_id=(dt, dy), device_id_type=MESH)

    greet(sib, y)
    for d in range(1, 4):
        greet(tm, yn[d])
        greet(sib, yn[d])
        greet(xn[d], y)
        greet(zn[d], y)
    gives = jnp.logical_and(h == 0, chip > 0)
    takes = chip < NX * NZ - 1
    down0, down1 = lax.max(tm - 2, 0), lax.max(tm - 1, 0)
    up = lax.min(2 * chip + 2, 2 * NX * NZ - 2)

    @pl.when(gives)
    def _():
        greet(down0, y)
        greet(down1, y)

    @pl.when(takes)
    def _():
        greet(up, y)

    def prep_w(p, slot):
        for a in range(A):
            for j in range(2):
                hi, lo = halves(wf[p, a, j])
                cs = pl.ds(128 * j, 128)
                rhs[slot, pl.ds(a * CH, CH), cs] = hi
                rhs[slot, pl.ds((A + a) * CH, CH), cs] = lo
                rhs[slot, pl.ds((2 * A + a) * CH, CH), cs] = hi

    def prep_x(i):
        for a in range(A):
            hi, lo = halves(xe[pl.ds(pl.multiple_of(R * h + 80 * i + 16 * a, 16), 80), :])
            rows = pl.ds(pl.multiple_of(80 * i, 16), 80)
            xcat[rows, pl.ds(a * CH, CH)] = hi
            xcat[rows, pl.ds((A + a) * CH, CH)] = hi
            xcat[rows, pl.ds((2 * A + a) * CH, CH)] = lo

    acc[...] = jnp.zeros_like(acc)
    zpad = jnp.zeros((16, K), F32)
    s_ext[pl.ds(0, 16)] = zpad
    s_ext[pl.ds(16 + PR, 16)] = zpad
    lx.wait()
    pl.loop(0, 12)(prep_x)
    for c in wcopies[:4]:
        c.wait()
    prep_w(0, 0)
    pl.semaphore_wait(bar, 13 + jnp.where(gives, 2, 0) + jnp.where(takes, 1, 0))

    kh0, kh1, ks0, ks1 = sem(), sem(), sem(), sem()
    halo = xe.at[pl.ds(PR, 64)]
    heads = [send(rec.at[pl.ds(0, 64)], xe.at[pl.ds(own0, 64)], ks0, sib, y),
             send(rec.at[pl.ds(64, R - 64)], xe.at[pl.ds(pl.multiple_of(own0 + 64, 64), R - 64)], ks1, sib, y)]
    halos = [pltpu.make_async_remote_copy(src_ref=rec.at[pl.ds(0, 64)], dst_ref=halo, send_sem=ss.at[kk],
                                          recv_sem=rs.at[kh0], device_id=(dd, y), device_id_type=MESH)
             for kk, dd in ((kh0, down0), (kh1, down1))]

    @pl.when(gives)
    def _():
        halos[0].start()
        halos[1].start()

    heads[0].start()
    heads[1].start()
    for c in wcopies[4:]:
        c.wait()
    oth0 = pl.multiple_of(R - R * h, R)
    outs = []

    def go(src, dst, k, dt, dy=y):
        c = send(src, dst, k, dt, dy)
        c.start()
        outs.append(c)

    kry = [sem() for _ in range(3)]
    ycopies = {d: send(acc.at[pl.ds(pl.multiple_of(yn[d] * 256, 256), 256)], ry.at[d - 1], kry[d - 1], tm, yn[d])
               for d in (2, 1, 3)}
    HR = R // 2
    for half in range(2):
        if half == 1:
            @pl.when(jnp.logical_not(takes))
            def _():
                halo[...] = jnp.zeros((64, CH), F32)

            @pl.when(takes)
            def _():
                arrived(halo, kh0)

            arrived(xe.at[pl.ds(oth0, 64)], ks0)
            prep_x(12)

        @pl.loop(0, 8)
        def _(p):
            slot = p % 2
            res = jnp.dot(xcat[pl.ds(HR * half, HR + 16)], rhs[slot], preferred_element_type=F32)
            yb[0] = res[:, :K]
            yb[1] = res[:, K:]
            prep_w((p + 1) % 8, 1 - slot)
            acc[pl.ds(HR * half, HR)] += yb[0, pl.ds(2 * p, HR), :] + yb[1, pl.ds(2 * p + 1, HR), :]

        for d in (2, 1, 3):
            pl.when(yn[d] // 2 == half)(ycopies[d].start)
    outs.extend(ycopies.values())
    arrived(xe.at[pl.ds(pl.multiple_of(oth0 + 64, 64), R - 64)], ks1)

    order = (2, 1, 3, 0)
    shift = [16 * ((x + o) % 4) for o in order]

    def xprep(i):
        cols = pl.multiple_of(128 * i, 128)
        for a in range(A):
            v = xe[pl.ds(pl.multiple_of(128 * i + shift[a], 16), 128), :].T
            hi, lo = halves(v)
            rows = pl.ds(a * CH, CH)
            xt[rows, pl.ds(cols, 128)] = hi
            xt[rows, pl.ds(pl.multiple_of(PR + cols, 128), 128)] = hi
            xt[rows, pl.ds(pl.multiple_of(2 * PR + cols, 128), 128)] = lo

    for a in range(A):
        v = xe[pl.ds(pl.multiple_of(PR + shift[a], 16), 16), :]
        hi = v.astype(BF16).astype(F32)
        t = jnp.concatenate([hi, hi, v - hi, jnp.zeros((80, CH), F32)], axis=0)
        xt[pl.ds(a * CH, CH), pl.ds(3 * PR, 128)] = t.T.astype(BF16)
    pl.loop(0, 8)(xprep)
    for d in range(1, 4):
        arrived(ry.at[d - 1], kry[d - 1])
    own_q = pl.ds(pl.multiple_of(y * 256, 256), 256)
    mine = pl.ds(pl.multiple_of(16 + R * h + 256 * y, 16), 256)
    s_ext[mine] = (acc[own_q] + ry[0]) + (ry[1] + ry[2])

    kag = [sem() for _ in range(3)]
    kfw = [sem() for _ in range(4)]
    kge = [sem() for _ in range(7)]
    kgx = [sem() for _ in range(3)]
    kgz = [sem() for _ in range(3)]
    kgb = [sem() for _ in range(7)]

    def place(hh, yy):
        return s_ext.at[pl.ds(pl.multiple_of(16 + R * hh + 256 * yy, 16), 256)]

    def piece(hh, yy):
        return pl.ds(pl.multiple_of((hh * NY + yy) * 16, 16), 16)

    sv = s_ext[mine]
    gm[...] = lax.dot_general(sv, sv, TN_DOT, precision=HI, preferred_element_type=F32)
    eight = [(0, 1), (0, 2), (0, 3), (1, 0), (1, 1), (1, 2), (1, 3)]
    hs, ts = (h, 1 - h), (tm, sib)
    for i, (o, d) in enumerate(eight):
        go(gm.at[piece(hs[o], yn[d])], ge.at[i], kge[i], ts[o], yn[d])
    go(place(h, y), place(h, y), kfw[0], sib)
    for d in (2, 1, 3):
        go(place(h, y), place(h, y), kag[d - 1], tm, yn[d])
    pl.loop(8, 16)(xprep)
    def forward(d):
        src = place(h, (y + 4 - d) % NY)
        arrived(src, kag[d - 1])
        go(src, src, kfw[d], sib)

    forward(1)
    forward(3)
    forward(2)
    for i in range(7):
        arrived(ge.at[i], kge[i])
    gm[piece(h, y)] = (((gm[piece(h, y)] + ge[0]) + (ge[1] + ge[2])) + ((ge[3] + ge[4]) + (ge[5] + ge[6])))
    for d in range(1, 4):
        go(gm.at[piece(h, y)], gx.at[d - 1], kgx[d - 1], xn[d])
    for d in range(4):
        arrived(place(1 - h, (y + 4 - d) % NY), kfw[d])

    def prep_s(n):
        for j in range(2):
            cs = pl.ds(128 * j, 128)
            off = 16 - j - 2 * h - 4 * ((z + order[n]) % NZ)
            hi, lo = halves(s_ext[pl.ds(off, PR), :])
            srhs[n, pl.ds(0, PR), cs] = hi
            srhs[n, pl.ds(PR, PR), cs] = lo
            srhs[n, pl.ds(2 * PR, PR), cs] = hi
            hi, lo = halves(s_ext[pl.ds(PR + off, 16), :])
            srhs[n, pl.ds(3 * PR, 16), cs] = hi
            srhs[n, pl.ds(3 * PR + 16, 16), cs] = lo
            srhs[n, pl.ds(3 * PR + 32, 16), cs] = hi
            srhs[n, pl.ds(3 * PR + 48, 80), cs] = jnp.zeros((80, K), BF16)

    def unit(u, c):
        rows = pl.ds(512 * u, 512)
        res = jnp.dot(xt[rows, :], srhs[c], preferred_element_type=F32)
        cp[c, rows, :] = res[:, :K]
        for m in range(2):
            cp[4 + 2 * u + m, pl.ds(256 * c, 256), :] = res[256 * m : 256 * m + 256, K:]

    rk = [[sem() for _ in range(6)] for _ in range(8)]

    def ends(n):
        return (xn[1], xn[3]) if n < 4 else (zn[1], zn[3])

    def first(i, *ns):
        for n in ns:
            up, dn = ends(n)
            src, buf = cp.at[n], xr.at[n]
            if i == 0:
                go(src.at[0:128], buf.at[0], rk[n][0], up)
                go(src.at[128:256], buf.at[1], rk[n][1], dn)
            elif i == 1:
                go(src.at[384:512], buf.at[3], rk[n][3], up)
            else:
                go(src.at[512:640], buf.at[2], rk[n][2], dn)

    def second_a(*ns):
        for n in ns:
            arrived(xr.at[n, 0], rk[n][0])
            cp[n, 256:384] += xr[n, 0]
            go(cp.at[n, 256:384], xr.at[n, 4], rk[n][4], ends(n)[0])

    def second_b(*ns):
        for n in ns:
            arrived(xr.at[n, 1], rk[n][1])
            cp[n, 640:768] += xr[n, 1]
            go(cp.at[n, 640:768], xr.at[n, 5], rk[n][5], ends(n)[1])

    def last(n, dst):
        for i in (2, 3, 4, 5):
            arrived(xr.at[n, i], rk[n][i])
        dst[0:128] = cp[n, 768:896] + (xr[n, 2] + xr[n, 4])
        dst[128:256] = cp[n, 896:1024] + (xr[n, 3] + xr[n, 5])

    zk = [[sem() for _ in range(6)] for _ in range(2)]

    def part_own(q, t, src):
        up, dn = ends(0 if q else 4)
        buf, ks = (pz, qz)[q], zk[q]
        a, b = src.at[0:128], src.at[128:256]
        if t == 0:
            go(a, buf.at[0], ks[0], up)
            go(b, buf.at[1], ks[1], dn)
        elif t == 1:
            go(b, buf.at[3], ks[3], up)
        else:
            go(a, buf.at[2], ks[2], dn)

    def part_on(q, t, src):
        up, dn = ends(0 if q else 4)
        buf, ks = (pz, qz)[q], zk[q]
        half, to = (pl.ds(0, 128), up) if t == 1 else (pl.ds(128, 128), dn)
        arrived(buf.at[t - 1], ks[t - 1])
        src[half] += buf[t - 1]
        go(src.at[half], buf.at[3 + t], ks[3 + t], to)

    def part_sum(q, src, dst):
        buf, ks = (pz, qz)[q], zk[q]
        for i in (2, 3, 4, 5):
            arrived(buf.at[i], ks[i])
        dst[0:128] = src[0:128] + (buf[2] + buf[4])
        dst[128:256] = src[128:256] + (buf[3] + buf[5])

    def p_last(n):
        last(n, p1.at[n])
        part_own(0, n, p1.at[n])

    def q_last(n):
        last(4 + n, q1.at[n])
        part_own(1, n, q1.at[n])

    prep_s(0)
    unit(0, 0)
    first(0, 0)
    first(1, 0)
    for d in range(1, 4):
        arrived(gx.at[d - 1], kgx[d - 1])
    gz[3] = (gm[piece(h, y)] + gx[0]) + (gx[1] + gx[2])
    for d in range(1, 4):
        go(gz.at[3], gz.at[d - 1], kgz[d - 1], zn[d])
    first(0, 4, 5)
    prep_s(1)
    unit(0, 1)
    first(0, 1)
    first(1, 1, 4, 5)
    for d in range(1, 4):
        arrived(gz.at[d - 1], kgz[d - 1])
    gb[piece(h, y)] = (gz[3] + gz[0]) + (gz[1] + gz[2])
    for i, (o, d) in enumerate(eight):
        go(gb.at[piece(h, y)], gb.at[piece(h, y)], kgb[i], ts[o], yn[d])
    prep_s(2)
    unit(1, 0)
    first(2, 0)
    first(0, 6, 7)
    second_a(0)
    second_b(0)
    for i, (o, d) in enumerate(eight):
        arrived(gb.at[piece(hs[o], (y + 4 - d) % NY)], kgb[i])
    gw[...] = gb[...]
    eye(li)
    prep_s(3)
    factor(gw, li, FAC[0])
    unit(1, 1)
    first(2, 1)
    first(1, 6, 7)
    second_a(1, 4, 5)
    second_b(1)
    factor(gw, li, FAC[1])
    unit(0, 2)
    first(0, 2)
    first(1, 2)
    first(2, 4, 5)
    second_b(4, 5)
    second_a(6, 7)
    factor(gw, li, FAC[2])
    unit(0, 3)
    first(0, 3)
    first(1, 3)
    p_last(0)
    p_last(1)
    factor(gw, li, FAC[3])
    unit(1, 2)
    first(2, 2, 6, 7)
    second_a(2)
    second_b(2, 6, 7)
    q_last(0)
    q_last(1)
    factor(gw, li, FAC[4])
    unit(1, 3)
    first(2, 3)
    second_a(3)
    second_b(3)
    part_on(0, 1, p1.at[1])
    part_on(1, 1, q1.at[1])
    s_o[...] = s_ext[pl.ds(pl.multiple_of(16 + R * h, 16), R), :]
    li_o[...] = li[...]
    p_last(2)
    part_on(0, 2, p1.at[2])
    q_last(2)
    part_on(1, 2, q1.at[2])
    last(3, p1.at[3])
    last(7, q1.at[3])
    part_sum(0, p1.at[3], raw.at[0])
    part_sum(1, q1.at[3], raw.at[1])

    for c in outs:
        c.wait_send()
    heads[0].wait_send()
    heads[1].wait_send()

    @pl.when(gives)
    def _():
        halos[0].wait_send()
        halos[1].wait_send()


FAC = (range(0, 3), range(3, 6), range(6, 9), range(9, 12), range(12, 16))


def apply_inverse(own, raw, inv, basis, coeffs):
    root = float(NX * NZ * PR) ** 0.5
    basis[...] = lax.dot_general(own[...], inv[...], NT_DOT, precision=HI, preferred_element_type=F32) * root
    for j in range(2):
        coeffs[j] = lax.dot_general(raw[j], inv[...], NT_DOT, precision=HI, preferred_element_type=F32)


def eye(li):
    rows = lax.broadcasted_iota(jnp.int32, (K, K), 0)
    cols = lax.broadcasted_iota(jnp.int32, (K, K), 1)
    li[...] = jnp.where(rows == cols, 1.0, 0.0).astype(F32)


def factor(g, li, blocks):
    for jb in blocks:
        base = 8 * jb
        rows = lax.broadcasted_iota(jnp.int32, (K - base, 1), 0)
        av, bv = g[base:], li[base:]
        for j in range(8):
            at_j = slice(base + j, base + j + 1)
            r = lax.rsqrt(av[j : j + 1, at_j])
            ra, rb = av[j : j + 1] * r, bv[j : j + 1] * r
            f = jnp.where(rows > j, av[:, at_j] * r, 0.0)
            av = av - f * ra
            bv = jnp.where(rows == j, rb, bv - f * rb)
        g[base:] = av
        li[base:] = bv


N_SEM = 4 + 3 + 3 + 4 + 48 + 12 + 7 + 3 + 3 + 7


def on_device(record, test_matrix):
    V = pl.BlockSpec(memory_space=pltpu.VMEM)
    H = pl.BlockSpec(memory_space=pl.ANY)
    own, raw, inv = pl.pallas_call(
        body,
        out_shape=(
            jax.ShapeDtypeStruct((R, K), F32),
            jax.ShapeDtypeStruct((2, CH, K), F32),
            jax.ShapeDtypeStruct((K, K), F32),
        ),
        in_specs=[H, H],
        out_specs=(V, V, V),
        scratch_shapes=[
            pltpu.VMEM((PR + 64, CH), F32),
            pltpu.VMEM((8, A, 2, CH, K), F32),
            pltpu.VMEM((R + 16, KC), BF16),
            pltpu.VMEM((2, KC, 2 * K), BF16),
            pltpu.VMEM((2, R // 2 + 16, K), F32),
            pltpu.VMEM((R, K), F32),
            pltpu.VMEM((3, 256, K), F32),
            pltpu.VMEM((PR + 32, K), F32),
            pltpu.VMEM((A * CH, KT), BF16),
            pltpu.VMEM((4, KT, 2 * K), BF16),
            pltpu.VMEM((8, A * CH, K), F32),
            pltpu.VMEM((8, 6, 128, K), F32),
            pltpu.VMEM((4, CH, K), F32),
            pltpu.VMEM((4, CH, K), F32),
            pltpu.VMEM((6, 128, K), F32),
            pltpu.VMEM((6, 128, K), F32),
            pltpu.VMEM((K, K), F32),
            pltpu.VMEM((7, 16, K), F32),
            pltpu.VMEM((3, 16, K), F32),
            pltpu.VMEM((4, 16, K), F32),
            pltpu.VMEM((K, K), F32),
            pltpu.VMEM((K, K), F32),
            pltpu.VMEM((K, K), F32),
            pltpu.SemaphoreType.DMA((33,)),
            pltpu.SemaphoreType.DMA((N_SEM,)),
            pltpu.SemaphoreType.DMA((N_SEM,)),
        ],
        compiler_params=pltpu.CompilerParams(collective_id=0, has_side_effects=True, vmem_limit_bytes=60 * 2**20),
    )(record, test_matrix)
    return pl.pallas_call(
        apply_inverse,
        out_shape=(jax.ShapeDtypeStruct((R, K), F32), jax.ShapeDtypeStruct((2, CH, K), F32)),
        in_specs=[V, V, V],
        out_specs=(V, V),
    )(own, raw, inv)


def solution(mesh):
    return jax.shard_map(
        on_device,
        mesh=mesh,
        in_specs=(P("tm", "chan"), P(None, "chan", None)),
        out_specs=(P("tm", None), P("tm", "chan", None)),
        check_vma=False,
    )
```

```python
import jax
import jax.numpy as jnp
from jax import lax
from jax.experimental import pallas as pl
from jax.experimental.pallas import tpu as pltpu
from jax.sharding import PartitionSpec as P

F32, BF16 = jnp.float32, jnp.bfloat16
MESH = pl.DeviceIdType.MESH
NX, NZ, NY = 4, 4, 4
LAGS, CH, K = 64, 256, 128
R = 1024
PR = 2 * R
A = 4
KC = 3 * A * CH
KT = 3 * PR + 128
NT_DOT = (((1,), (1,)), ((), ()))
TN_DOT = (((0,), (0,)), ((), ()))
HI = lax.Precision.HIGHEST


def halves(v):
    hi = v.astype(BF16)
    return hi, (v - hi.astype(F32)).astype(BF16)


def body(rec, w, s_o, raw, li_o, xe, wf, xcat, rhs, yb, acc, ry, s_ext, xt, srhs, cp,
         xr, p1, q1, pz, qz, gm, ge, gx, gz, gb, gw, li, lsem, ss, rs):
    tm = lax.axis_index("tm")
    y = lax.axis_index("chan")
    h = tm % 2
    chip = tm // 2
    z = chip % NZ
    x = chip // NZ

    def at(xx, zz, hh):
        return (xx * NZ + zz) * 2 + hh

    sib = at(x, z, 1 - h)
    xn = [at((x + d) % NX, z, h) for d in range(NX)]
    zn = [at(x, (z + d) % NZ, h) for d in range(NZ)]
    yn = [(y + d) % NY for d in range(NY)]

    def send(src, dst, k, dt, dy):
        return pltpu.make_async_remote_copy(src_ref=src, dst_ref=dst, send_sem=ss.at[k], recv_sem=rs.at[k],
                                            device_id=(dt, dy), device_id_type=MESH)

    def arrived(ref, k):
        send(ref, ref, k, sib, y).wait_recv()

    count = [0]

    def sem():
        count[0] += 1
        return count[0] - 1

    own0 = pl.multiple_of(R * h, R)
    lx = pltpu.make_async_copy(rec, xe.at[pl.ds(own0, R)], lsem.at[0])
    lx.start()
    wcopies = []
    for p in range(8):
        for a in range(A):
            c = pltpu.make_async_copy(w.at[pl.ds(16 * a + 2 * p, 2)], wf.at[p, a], lsem.at[1 + 4 * p + a])
            c.start()
            wcopies.append(c)

    bar = pltpu.get_barrier_semaphore()

    def greet(dt, dy):
        pl.semaphore_signal(bar, inc=1, device_id=(dt, dy), device_id_type=MESH)

    greet(sib, y)
    for d in range(1, 4):
        greet(tm, yn[d])
        greet(sib, yn[d])
        greet(xn[d], y)
        greet(zn[d], y)
    gives = jnp.logical_and(h == 0, chip > 0)
    takes = chip < NX * NZ - 1
    down0, down1 = lax.max(tm - 2, 0), lax.max(tm - 1, 0)
    up = lax.min(2 * chip + 2, 2 * NX * NZ - 2)

    @pl.when(gives)
    def _():
        greet(down0, y)
        greet(down1, y)

    @pl.when(takes)
    def _():
        greet(up, y)

    def prep_w(p, slot):
        for a in range(A):
            for j in range(2):
                hi, lo = halves(wf[p, a, j])
                cs = pl.ds(128 * j, 128)
                rhs[slot, pl.ds(a * CH, CH), cs] = hi
                rhs[slot, pl.ds((A + a) * CH, CH), cs] = lo
                rhs[slot, pl.ds((2 * A + a) * CH, CH), cs] = hi

    def prep_x(i):
        for a in range(A):
            hi, lo = halves(xe[pl.ds(pl.multiple_of(R * h + 80 * i + 16 * a, 16), 80), :])
            rows = pl.ds(pl.multiple_of(80 * i, 16), 80)
            xcat[rows, pl.ds(a * CH, CH)] = hi
            xcat[rows, pl.ds((A + a) * CH, CH)] = hi
            xcat[rows, pl.ds((2 * A + a) * CH, CH)] = lo

    acc[...] = jnp.zeros_like(acc)
    zpad = jnp.zeros((16, K), F32)
    s_ext[pl.ds(0, 16)] = zpad
    s_ext[pl.ds(16 + PR, 16)] = zpad
    lx.wait()
    pl.loop(0, 12)(prep_x)
    for c in wcopies[:4]:
        c.wait()
    prep_w(0, 0)
    pl.semaphore_wait(bar, 13 + jnp.where(gives, 2, 0) + jnp.where(takes, 1, 0))

    kh0, kh1, ks0, ks1 = sem(), sem(), sem(), sem()
    halo = xe.at[pl.ds(PR, 64)]
    heads = [send(rec.at[pl.ds(0, 64)], xe.at[pl.ds(own0, 64)], ks0, sib, y),
             send(rec.at[pl.ds(64, R - 64)], xe.at[pl.ds(pl.multiple_of(own0 + 64, 64), R - 64)], ks1, sib, y)]
    halos = [pltpu.make_async_remote_copy(src_ref=rec.at[pl.ds(0, 64)], dst_ref=halo, send_sem=ss.at[kk],
                                          recv_sem=rs.at[kh0], device_id=(dd, y), device_id_type=MESH)
             for kk, dd in ((kh0, down0), (kh1, down1))]

    @pl.when(gives)
    def _():
        halos[0].start()
        halos[1].start()

    heads[0].start()
    heads[1].start()
    for c in wcopies[4:]:
        c.wait()
    oth0 = pl.multiple_of(R - R * h, R)
    outs = []

    def go(src, dst, k, dt, dy=y):
        c = send(src, dst, k, dt, dy)
        c.start()
        outs.append(c)

    kry = [sem() for _ in range(3)]
    ycopies = {d: send(acc.at[pl.ds(pl.multiple_of(yn[d] * 256, 256), 256)], ry.at[d - 1], kry[d - 1], tm, yn[d])
               for d in (2, 1, 3)}
    HR = R // 2
    for half in range(2):
        if half == 1:
            @pl.when(jnp.logical_not(takes))
            def _():
                halo[...] = jnp.zeros((64, CH), F32)

            @pl.when(takes)
            def _():
                arrived(halo, kh0)

            arrived(xe.at[pl.ds(oth0, 64)], ks0)
            prep_x(12)

        @pl.loop(0, 8)
        def _(p):
            slot = p % 2
            res = jnp.dot(xcat[pl.ds(HR * half, HR + 16)], rhs[slot], preferred_element_type=F32)
            yb[0] = res[:, :K]
            yb[1] = res[:, K:]
            prep_w((p + 1) % 8, 1 - slot)
            acc[pl.ds(HR * half, HR)] += yb[0, pl.ds(2 * p, HR), :] + yb[1, pl.ds(2 * p + 1, HR), :]

        for d in (2, 1, 3):
            pl.when(yn[d] // 2 == half)(ycopies[d].start)
    outs.extend(ycopies.values())
    arrived(xe.at[pl.ds(pl.multiple_of(oth0 + 64, 64), R - 64)], ks1)

    order = (2, 1, 3, 0)
    shift = [16 * ((x + o) % 4) for o in order]

    def xprep(i):
        cols = pl.multiple_of(128 * i, 128)
        for a in range(A):
            v = xe[pl.ds(pl.multiple_of(128 * i + shift[a], 16), 128), :].T
            hi, lo = halves(v)
            rows = pl.ds(a * CH, CH)
            xt[rows, pl.ds(cols, 128)] = hi
            xt[rows, pl.ds(pl.multiple_of(PR + cols, 128), 128)] = hi
            xt[rows, pl.ds(pl.multiple_of(2 * PR + cols, 128), 128)] = lo

    for a in range(A):
        v = xe[pl.ds(pl.multiple_of(PR + shift[a], 16), 16), :]
        hi = v.astype(BF16).astype(F32)
        t = jnp.concatenate([hi, hi, v - hi, jnp.zeros((80, CH), F32)], axis=0)
        xt[pl.ds(a * CH, CH), pl.ds(3 * PR, 128)] = t.T.astype(BF16)
    pl.loop(0, 8)(xprep)
    for d in range(1, 4):
        arrived(ry.at[d - 1], kry[d - 1])
    own_q = pl.ds(pl.multiple_of(y * 256, 256), 256)
    mine = pl.ds(pl.multiple_of(16 + R * h + 256 * y, 16), 256)
    s_ext[mine] = (acc[own_q] + ry[0]) + (ry[1] + ry[2])

    kag = [sem() for _ in range(3)]
    kfw = [sem() for _ in range(4)]
    kge = [sem() for _ in range(7)]
    kgx = [sem() for _ in range(3)]
    kgz = [sem() for _ in range(3)]
    kgb = [sem() for _ in range(7)]

    def place(hh, yy):
        return s_ext.at[pl.ds(pl.multiple_of(16 + R * hh + 256 * yy, 16), 256)]

    def piece(hh, yy):
        return pl.ds(pl.multiple_of((hh * NY + yy) * 16, 16), 16)

    sv = s_ext[mine]
    gm[...] = lax.dot_general(sv, sv, TN_DOT, precision=HI, preferred_element_type=F32)
    eight = [(0, 1), (0, 2), (0, 3), (1, 0), (1, 1), (1, 2), (1, 3)]
    hs, ts = (h, 1 - h), (tm, sib)
    for i, (o, d) in enumerate(eight):
        go(gm.at[piece(hs[o], yn[d])], ge.at[i], kge[i], ts[o], yn[d])
    go(place(h, y), place(h, y), kfw[0], sib)
    for d in (2, 1, 3):
        go(place(h, y), place(h, y), kag[d - 1], tm, yn[d])
    pl.loop(8, 16)(xprep)
    def forward(d):
        src = place(h, (y + 4 - d) % NY)
        arrived(src, kag[d - 1])
        go(src, src, kfw[d], sib)

    forward(1)
    forward(3)
    forward(2)
    for i in range(7):
        arrived(ge.at[i], kge[i])
    gm[piece(h, y)] = (((gm[piece(h, y)] + ge[0]) + (ge[1] + ge[2])) + ((ge[3] + ge[4]) + (ge[5] + ge[6])))
    for d in range(1, 4):
        go(gm.at[piece(h, y)], gx.at[d - 1], kgx[d - 1], xn[d])
    for d in range(4):
        arrived(place(1 - h, (y + 4 - d) % NY), kfw[d])

    def prep_s(n):
        for j in range(2):
            cs = pl.ds(128 * j, 128)
            off = 16 - j - 2 * h - 4 * ((z + order[n]) % NZ)
            hi, lo = halves(s_ext[pl.ds(off, PR), :])
            srhs[n, pl.ds(0, PR), cs] = hi
            srhs[n, pl.ds(PR, PR), cs] = lo
            srhs[n, pl.ds(2 * PR, PR), cs] = hi
            hi, lo = halves(s_ext[pl.ds(PR + off, 16), :])
            srhs[n, pl.ds(3 * PR, 16), cs] = hi
            srhs[n, pl.ds(3 * PR + 16, 16), cs] = lo
            srhs[n, pl.ds(3 * PR + 32, 16), cs] = hi
            srhs[n, pl.ds(3 * PR + 48, 80), cs] = jnp.zeros((80, K), BF16)

    def unit(u, c):
        rows = pl.ds(512 * u, 512)
        res = jnp.dot(xt[rows, :], srhs[c], preferred_element_type=F32)
        cp[c, rows, :] = res[:, :K]
        for m in range(2):
            cp[4 + 2 * u + m, pl.ds(256 * c, 256), :] = res[256 * m : 256 * m + 256, K:]

    rk = [[sem() for _ in range(6)] for _ in range(8)]

    def ends(n):
        return (xn[1], xn[3]) if n < 4 else (zn[1], zn[3])

    def first(i, *ns):
        for n in ns:
            up, dn = ends(n)
            src, buf = cp.at[n], xr.at[n]
            if i == 0:
                go(src.at[0:128], buf.at[0], rk[n][0], up)
                go(src.at[128:256], buf.at[1], rk[n][1], dn)
            elif i == 1:
                go(src.at[384:512], buf.at[3], rk[n][3], up)
            else:
                go(src.at[512:640], buf.at[2], rk[n][2], dn)

    def second_a(*ns):
        for n in ns:
            arrived(xr.at[n, 0], rk[n][0])
            cp[n, 256:384] += xr[n, 0]
            go(cp.at[n, 256:384], xr.at[n, 4], rk[n][4], ends(n)[0])

    def second_b(*ns):
        for n in ns:
            arrived(xr.at[n, 1], rk[n][1])
            cp[n, 640:768] += xr[n, 1]
            go(cp.at[n, 640:768], xr.at[n, 5], rk[n][5], ends(n)[1])

    def last(n, dst):
        for i in (2, 3, 4, 5):
            arrived(xr.at[n, i], rk[n][i])
        dst[0:128] = cp[n, 768:896] + (xr[n, 2] + xr[n, 4])
        dst[128:256] = cp[n, 896:1024] + (xr[n, 3] + xr[n, 5])

    zk = [[sem() for _ in range(6)] for _ in range(2)]

    def part_own(q, t, src):
        up, dn = ends(0 if q else 4)
        buf, ks = (pz, qz)[q], zk[q]
        a, b = src.at[0:128], src.at[128:256]
        if t == 0:
            go(a, buf.at[0], ks[0], up)
            go(b, buf.at[1], ks[1], dn)
        elif t == 1:
            go(b, buf.at[3], ks[3], up)
        else:
            go(a, buf.at[2], ks[2], dn)

    def part_on(q, t, src):
        up, dn = ends(0 if q else 4)
        buf, ks = (pz, qz)[q], zk[q]
        half, to = (pl.ds(0, 128), up) if t == 1 else (pl.ds(128, 128), dn)
        arrived(buf.at[t - 1], ks[t - 1])
        src[half] += buf[t - 1]
        go(src.at[half], buf.at[3 + t], ks[3 + t], to)

    def part_sum(q, src, dst):
        buf, ks = (pz, qz)[q], zk[q]
        for i in (2, 3, 4, 5):
            arrived(buf.at[i], ks[i])
        dst[0:128] = src[0:128] + (buf[2] + buf[4])
        dst[128:256] = src[128:256] + (buf[3] + buf[5])

    def p_last(n):
        last(n, p1.at[n])
        part_own(0, n, p1.at[n])

    def q_last(n):
        last(4 + n, q1.at[n])
        part_own(1, n, q1.at[n])

    prep_s(0)
    unit(0, 0)
    first(0, 0)
    first(1, 0)
    for d in range(1, 4):
        arrived(gx.at[d - 1], kgx[d - 1])
    gz[3] = (gm[piece(h, y)] + gx[0]) + (gx[1] + gx[2])
    for d in range(1, 4):
        go(gz.at[3], gz.at[d - 1], kgz[d - 1], zn[d])
    first(0, 4, 5)
    prep_s(1)
    unit(0, 1)
    first(0, 1)
    first(1, 1, 4, 5)
    for d in range(1, 4):
        arrived(gz.at[d - 1], kgz[d - 1])
    gb[piece(h, y)] = (gz[3] + gz[0]) + (gz[1] + gz[2])
    for i, (o, d) in enumerate(eight):
        go(gb.at[piece(h, y)], gb.at[piece(h, y)], kgb[i], ts[o], yn[d])
    prep_s(2)
    unit(1, 0)
    first(2, 0)
    first(0, 6, 7)
    second_a(0)
    second_b(0)
    for i, (o, d) in enumerate(eight):
        arrived(gb.at[piece(hs[o], (y + 4 - d) % NY)], kgb[i])
    gw[...] = gb[...]
    eye(li)
    prep_s(3)
    factor(gw, li, FAC[0])
    unit(1, 1)
    first(2, 1)
    first(1, 6, 7)
    second_a(1, 4, 5)
    second_b(1)
    factor(gw, li, FAC[1])
    unit(0, 2)
    first(0, 2)
    first(1, 2)
    first(2, 4, 5)
    second_b(4, 5)
    second_a(6, 7)
    factor(gw, li, FAC[2])
    unit(0, 3)
    first(0, 3)
    first(1, 3)
    p_last(0)
    p_last(1)
    factor(gw, li, FAC[3])
    unit(1, 2)
    first(2, 2, 6, 7)
    second_a(2)
    second_b(2, 6, 7)
    q_last(0)
    q_last(1)
    factor(gw, li, FAC[4])
    unit(1, 3)
    first(2, 3)
    second_a(3)
    second_b(3)
    p_last(2)
    q_last(2)
    part_on(0, 1, p1.at[1])
    part_on(1, 1, q1.at[1])
    part_on(0, 2, p1.at[2])
    part_on(1, 2, q1.at[2])
    s_o[...] = s_ext[pl.ds(pl.multiple_of(16 + R * h, 16), R), :]
    li_o[...] = li[...]
    last(3, p1.at[3])
    last(7, q1.at[3])
    part_sum(0, p1.at[3], raw.at[0])
    part_sum(1, q1.at[3], raw.at[1])

    for c in outs:
        c.wait_send()
    heads[0].wait_send()
    heads[1].wait_send()

    @pl.when(gives)
    def _():
        halos[0].wait_send()
        halos[1].wait_send()


FAC = (range(0, 3), range(3, 6), range(6, 9), range(9, 12), range(12, 16))


def apply_inverse(own, raw, inv, basis, coeffs):
    root = float(NX * NZ * PR) ** 0.5
    basis[...] = lax.dot_general(own[...], inv[...], NT_DOT, precision=HI, preferred_element_type=F32) * root
    for j in range(2):
        coeffs[j] = lax.dot_general(raw[j], inv[...], NT_DOT, precision=HI, preferred_element_type=F32)


def eye(li):
    rows = lax.broadcasted_iota(jnp.int32, (K, K), 0)
    cols = lax.broadcasted_iota(jnp.int32, (K, K), 1)
    li[...] = jnp.where(rows == cols, 1.0, 0.0).astype(F32)


def factor(g, li, blocks):
    for jb in blocks:
        base = 8 * jb
        rows = lax.broadcasted_iota(jnp.int32, (K - base, 1), 0)
        av, bv = g[base:], li[base:]
        for j in range(8):
            at_j = slice(base + j, base + j + 1)
            r = lax.rsqrt(av[j : j + 1, at_j])
            ra, rb = av[j : j + 1] * r, bv[j : j + 1] * r
            f = jnp.where(rows > j, av[:, at_j] * r, 0.0)
            av = av - f * ra
            bv = jnp.where(rows == j, rb, bv - f * rb)
        g[base:] = av
        li[base:] = bv


N_SEM = 4 + 3 + 3 + 4 + 48 + 12 + 7 + 3 + 3 + 7


def on_device(record, test_matrix):
    V = pl.BlockSpec(memory_space=pltpu.VMEM)
    H = pl.BlockSpec(memory_space=pl.ANY)
    own, raw, inv = pl.pallas_call(
        body,
        out_shape=(
            jax.ShapeDtypeStruct((R, K), F32),
            jax.ShapeDtypeStruct((2, CH, K), F32),
            jax.ShapeDtypeStruct((K, K), F32),
        ),
        in_specs=[H, H],
        out_specs=(V, V, V),
        scratch_shapes=[
            pltpu.VMEM((PR + 64, CH), F32),
            pltpu.VMEM((8, A, 2, CH, K), F32),
            pltpu.VMEM((R + 16, KC), BF16),
            pltpu.VMEM((2, KC, 2 * K), BF16),
            pltpu.VMEM((2, R // 2 + 16, K), F32),
            pltpu.VMEM((R, K), F32),
            pltpu.VMEM((3, 256, K), F32),
            pltpu.VMEM((PR + 32, K), F32),
            pltpu.VMEM((A * CH, KT), BF16),
            pltpu.VMEM((4, KT, 2 * K), BF16),
            pltpu.VMEM((8, A * CH, K), F32),
            pltpu.VMEM((8, 6, 128, K), F32),
            pltpu.VMEM((4, CH, K), F32),
            pltpu.VMEM((4, CH, K), F32),
            pltpu.VMEM((6, 128, K), F32),
            pltpu.VMEM((6, 128, K), F32),
            pltpu.VMEM((K, K), F32),
            pltpu.VMEM((7, 16, K), F32),
            pltpu.VMEM((3, 16, K), F32),
            pltpu.VMEM((4, 16, K), F32),
            pltpu.VMEM((K, K), F32),
            pltpu.VMEM((K, K), F32),
            pltpu.VMEM((K, K), F32),
            pltpu.SemaphoreType.DMA((33,)),
            pltpu.SemaphoreType.DMA((N_SEM,)),
            pltpu.SemaphoreType.DMA((N_SEM,)),
        ],
        compiler_params=pltpu.CompilerParams(collective_id=0, has_side_effects=True, vmem_limit_bytes=60 * 2**20),
    )(record, test_matrix)
    return pl.pallas_call(
        apply_inverse,
        out_shape=(jax.ShapeDtypeStruct((R, K), F32), jax.ShapeDtypeStruct((2, CH, K), F32)),
        in_specs=[V, V, V],
        out_specs=(V, V),
    )(own, raw, inv)


def solution(mesh):
    return jax.shard_map(
        on_device,
        mesh=mesh,
        in_specs=(P("tm", "chan"), P(None, "chan", None)),
        out_specs=(P("tm", None), P("tm", "chan", None)),
        check_vma=False,
    )
```

```python
import jax
import jax.numpy as jnp
from jax import lax
from jax.experimental import pallas as pl
from jax.experimental.pallas import tpu as pltpu
from jax.sharding import PartitionSpec as P

F32, BF16 = jnp.float32, jnp.bfloat16
MESH = pl.DeviceIdType.MESH
NX, NZ, NY = 4, 4, 4
LAGS, CH, K = 64, 256, 128
R = 1024
PR = 2 * R
A = 4
KC = 3 * A * CH
KT = 3 * PR + 128
NT_DOT = (((1,), (1,)), ((), ()))
TN_DOT = (((0,), (0,)), ((), ()))
HI = lax.Precision.HIGHEST


def halves(v):
    hi = v.astype(BF16)
    return hi, (v - hi.astype(F32)).astype(BF16)


def body(rec, w, s_o, raw, li_o, xe, wf, xcat, rhs, yb, acc, ry, s_ext, xt, srhs, cp,
         xr, p1, q1, pz, qz, gm, ge, gx, gz, gb, gw, li, lsem, ss, rs):
    tm = lax.axis_index("tm")
    y = lax.axis_index("chan")
    h = tm % 2
    chip = tm // 2
    z = chip % NZ
    x = chip // NZ

    def at(xx, zz, hh):
        return (xx * NZ + zz) * 2 + hh

    sib = at(x, z, 1 - h)
    xn = [at((x + d) % NX, z, h) for d in range(NX)]
    zn = [at(x, (z + d) % NZ, h) for d in range(NZ)]
    yn = [(y + d) % NY for d in range(NY)]

    def send(src, dst, k, dt, dy):
        return pltpu.make_async_remote_copy(src_ref=src, dst_ref=dst, send_sem=ss.at[k], recv_sem=rs.at[k],
                                            device_id=(dt, dy), device_id_type=MESH)

    def arrived(ref, k):
        send(ref, ref, k, sib, y).wait_recv()

    count = [0]

    def sem():
        count[0] += 1
        return count[0] - 1

    own0 = pl.multiple_of(R * h, R)
    lx = pltpu.make_async_copy(rec, xe.at[pl.ds(own0, R)], lsem.at[0])
    lx.start()
    wcopies = []
    for p in range(8):
        for a in range(A):
            c = pltpu.make_async_copy(w.at[pl.ds(16 * a + 2 * p, 2)], wf.at[p, a], lsem.at[1 + 4 * p + a])
            c.start()
            wcopies.append(c)

    bar = pltpu.get_barrier_semaphore()

    def greet(dt, dy):
        pl.semaphore_signal(bar, inc=1, device_id=(dt, dy), device_id_type=MESH)

    greet(sib, y)
    for d in range(1, 4):
        greet(tm, yn[d])
        greet(sib, yn[d])
        greet(xn[d], y)
        greet(zn[d], y)
    gives = jnp.logical_and(h == 0, chip > 0)
    takes = chip < NX * NZ - 1
    down0, down1 = lax.max(tm - 2, 0), lax.max(tm - 1, 0)
    up = lax.min(2 * chip + 2, 2 * NX * NZ - 2)

    @pl.when(gives)
    def _():
        greet(down0, y)
        greet(down1, y)

    @pl.when(takes)
    def _():
        greet(up, y)

    def prep_w(p, slot):
        for a in range(A):
            for j in range(2):
                hi, lo = halves(wf[p, a, j])
                cs = pl.ds(128 * j, 128)
                rhs[slot, pl.ds(a * CH, CH), cs] = hi
                rhs[slot, pl.ds((A + a) * CH, CH), cs] = lo
                rhs[slot, pl.ds((2 * A + a) * CH, CH), cs] = hi

    def prep_x(i):
        for a in range(A):
            hi, lo = halves(xe[pl.ds(pl.multiple_of(R * h + 80 * i + 16 * a, 16), 80), :])
            rows = pl.ds(pl.multiple_of(80 * i, 16), 80)
            xcat[rows, pl.ds(a * CH, CH)] = hi
            xcat[rows, pl.ds((A + a) * CH, CH)] = hi
            xcat[rows, pl.ds((2 * A + a) * CH, CH)] = lo

    acc[...] = jnp.zeros_like(acc)
    zpad = jnp.zeros((16, K), F32)
    s_ext[pl.ds(0, 16)] = zpad
    s_ext[pl.ds(16 + PR, 16)] = zpad
    lx.wait()
    pl.loop(0, 12)(prep_x)
    for c in wcopies[:4]:
        c.wait()
    prep_w(0, 0)
    pl.semaphore_wait(bar, 13 + jnp.where(gives, 2, 0) + jnp.where(takes, 1, 0))

    kh0, kh1, ks0, ks1 = sem(), sem(), sem(), sem()
    halo = xe.at[pl.ds(PR, 64)]
    heads = [send(rec.at[pl.ds(0, 64)], xe.at[pl.ds(own0, 64)], ks0, sib, y),
             send(rec.at[pl.ds(64, R - 64)], xe.at[pl.ds(pl.multiple_of(own0 + 64, 64), R - 64)], ks1, sib, y)]
    halos = [pltpu.make_async_remote_copy(src_ref=rec.at[pl.ds(0, 64)], dst_ref=halo, send_sem=ss.at[kk],
                                          recv_sem=rs.at[kh0], device_id=(dd, y), device_id_type=MESH)
             for kk, dd in ((kh0, down0), (kh1, down1))]

    @pl.when(gives)
    def _():
        halos[0].start()
        halos[1].start()

    heads[0].start()
    heads[1].start()
    for c in wcopies[4:]:
        c.wait()
    oth0 = pl.multiple_of(R - R * h, R)
    outs = []

    def go(src, dst, k, dt, dy=y):
        c = send(src, dst, k, dt, dy)
        c.start()
        outs.append(c)

    kry = [sem() for _ in range(3)]
    ycopies = {d: send(acc.at[pl.ds(pl.multiple_of(yn[d] * 256, 256), 256)], ry.at[d - 1], kry[d - 1], tm, yn[d])
               for d in (2, 1, 3)}
    HR = R // 2
    for half in range(2):
        if half == 1:
            @pl.when(jnp.logical_not(takes))
            def _():
                halo[...] = jnp.zeros((64, CH), F32)

            @pl.when(takes)
            def _():
                arrived(halo, kh0)

            arrived(xe.at[pl.ds(oth0, 64)], ks0)
            prep_x(12)

        @pl.loop(0, 4)
        def _(pp):
            for slot in range(2):
                p = 2 * pp + slot
                res = jnp.dot(xcat[pl.ds(HR * half, HR + 16)], rhs[slot], preferred_element_type=F32)
                yb[2 * slot] = res[:, :K]
                yb[2 * slot + 1] = res[:, K:]
                prep_w((p + 1) % 8, 1 - slot)
                acc[pl.ds(HR * half, HR)] += yb[2 * slot, pl.ds(2 * p, HR), :] + yb[2 * slot + 1, pl.ds(2 * p + 1, HR), :]

        for d in (2, 1, 3):
            pl.when(yn[d] // 2 == half)(ycopies[d].start)
    outs.extend(ycopies.values())
    arrived(xe.at[pl.ds(pl.multiple_of(oth0 + 64, 64), R - 64)], ks1)

    order = (2, 1, 3, 0)
    shift = [16 * ((x + o) % 4) for o in order]

    def xprep(i):
        cols = pl.multiple_of(128 * i, 128)
        for a in range(A):
            v = xe[pl.ds(pl.multiple_of(128 * i + shift[a], 16), 128), :].T
            hi, lo = halves(v)
            rows = pl.ds(a * CH, CH)
            xt[rows, pl.ds(cols, 128)] = hi
            xt[rows, pl.ds(pl.multiple_of(PR + cols, 128), 128)] = hi
            xt[rows, pl.ds(pl.multiple_of(2 * PR + cols, 128), 128)] = lo

    for a in range(A):
        v = xe[pl.ds(pl.multiple_of(PR + shift[a], 16), 16), :]
        hi = v.astype(BF16).astype(F32)
        t = jnp.concatenate([hi, hi, v - hi, jnp.zeros((80, CH), F32)], axis=0)
        xt[pl.ds(a * CH, CH), pl.ds(3 * PR, 128)] = t.T.astype(BF16)
    pl.loop(0, 8)(xprep)
    for d in range(1, 4):
        arrived(ry.at[d - 1], kry[d - 1])
    own_q = pl.ds(pl.multiple_of(y * 256, 256), 256)
    mine = pl.ds(pl.multiple_of(16 + R * h + 256 * y, 16), 256)
    s_ext[mine] = (acc[own_q] + ry[0]) + (ry[1] + ry[2])

    kag = [sem() for _ in range(3)]
    kfw = [sem() for _ in range(4)]
    kge = [sem() for _ in range(7)]
    kgx = [sem() for _ in range(3)]
    kgz = [sem() for _ in range(3)]
    kgb = [sem() for _ in range(7)]

    def place(hh, yy):
        return s_ext.at[pl.ds(pl.multiple_of(16 + R * hh + 256 * yy, 16), 256)]

    def piece(hh, yy):
        return pl.ds(pl.multiple_of((hh * NY + yy) * 16, 16), 16)

    sv = s_ext[mine]
    gm[...] = lax.dot_general(sv, sv, TN_DOT, precision=HI, preferred_element_type=F32)
    eight = [(0, 1), (0, 2), (0, 3), (1, 0), (1, 1), (1, 2), (1, 3)]
    hs, ts = (h, 1 - h), (tm, sib)
    for i, (o, d) in enumerate(eight):
        go(gm.at[piece(hs[o], yn[d])], ge.at[i], kge[i], ts[o], yn[d])
    go(place(h, y), place(h, y), kfw[0], sib)
    for d in (2, 1, 3):
        go(place(h, y), place(h, y), kag[d - 1], tm, yn[d])
    pl.loop(8, 16)(xprep)
    def forward(d):
        src = place(h, (y + 4 - d) % NY)
        arrived(src, kag[d - 1])
        go(src, src, kfw[d], sib)

    forward(1)
    forward(3)
    forward(2)
    for i in range(7):
        arrived(ge.at[i], kge[i])
    gm[piece(h, y)] = (((gm[piece(h, y)] + ge[0]) + (ge[1] + ge[2])) + ((ge[3] + ge[4]) + (ge[5] + ge[6])))
    for d in range(1, 4):
        go(gm.at[piece(h, y)], gx.at[d - 1], kgx[d - 1], xn[d])
    for d in range(4):
        arrived(place(1 - h, (y + 4 - d) % NY), kfw[d])

    def prep_s(n):
        for j in range(2):
            cs = pl.ds(128 * j, 128)
            off = 16 - j - 2 * h - 4 * ((z + order[n]) % NZ)
            hi, lo = halves(s_ext[pl.ds(off, PR), :])
            srhs[n, pl.ds(0, PR), cs] = hi
            srhs[n, pl.ds(PR, PR), cs] = lo
            srhs[n, pl.ds(2 * PR, PR), cs] = hi
            hi, lo = halves(s_ext[pl.ds(PR + off, 16), :])
            srhs[n, pl.ds(3 * PR, 16), cs] = hi
            srhs[n, pl.ds(3 * PR + 16, 16), cs] = lo
            srhs[n, pl.ds(3 * PR + 32, 16), cs] = hi
            srhs[n, pl.ds(3 * PR + 48, 80), cs] = jnp.zeros((80, K), BF16)

    def unit(u, c):
        rows = pl.ds(512 * u, 512)
        res = jnp.dot(xt[rows, :], srhs[c], preferred_element_type=F32)
        cp[c, rows, :] = res[:, :K]
        for m in range(2):
            cp[4 + 2 * u + m, pl.ds(256 * c, 256), :] = res[256 * m : 256 * m + 256, K:]

    rk = [[sem() for _ in range(6)] for _ in range(8)]

    def ends(n):
        return (xn[1], xn[3]) if n < 4 else (zn[1], zn[3])

    def first(i, *ns):
        for n in ns:
            up, dn = ends(n)
            src, buf = cp.at[n], xr.at[n]
            if i == 0:
                go(src.at[0:128], buf.at[0], rk[n][0], up)
                go(src.at[128:256], buf.at[1], rk[n][1], dn)
            elif i == 1:
                go(src.at[384:512], buf.at[3], rk[n][3], up)
            else:
                go(src.at[512:640], buf.at[2], rk[n][2], dn)

    def second_a(*ns):
        for n in ns:
            arrived(xr.at[n, 0], rk[n][0])
            cp[n, 256:384] += xr[n, 0]
            go(cp.at[n, 256:384], xr.at[n, 4], rk[n][4], ends(n)[0])

    def second_b(*ns):
        for n in ns:
            arrived(xr.at[n, 1], rk[n][1])
            cp[n, 640:768] += xr[n, 1]
            go(cp.at[n, 640:768], xr.at[n, 5], rk[n][5], ends(n)[1])

    def last(n, dst):
        for i in (2, 3, 4, 5):
            arrived(xr.at[n, i], rk[n][i])
        dst[0:128] = cp[n, 768:896] + (xr[n, 2] + xr[n, 4])
        dst[128:256] = cp[n, 896:1024] + (xr[n, 3] + xr[n, 5])

    zk = [[sem() for _ in range(6)] for _ in range(2)]

    def part_own(q, t, src):
        up, dn = ends(0 if q else 4)
        buf, ks = (pz, qz)[q], zk[q]
        a, b = src.at[0:128], src.at[128:256]
        if t == 0:
            go(a, buf.at[0], ks[0], up)
            go(b, buf.at[1], ks[1], dn)
        elif t == 1:
            go(b, buf.at[3], ks[3], up)
        else:
            go(a, buf.at[2], ks[2], dn)

    def part_on(q, t, src):
        up, dn = ends(0 if q else 4)
        buf, ks = (pz, qz)[q], zk[q]
        half, to = (pl.ds(0, 128), up) if t == 1 else (pl.ds(128, 128), dn)
        arrived(buf.at[t - 1], ks[t - 1])
        src[half] += buf[t - 1]
        go(src.at[half], buf.at[3 + t], ks[3 + t], to)

    def part_sum(q, src, dst):
        buf, ks = (pz, qz)[q], zk[q]
        for i in (2, 3, 4, 5):
            arrived(buf.at[i], ks[i])
        dst[0:128] = src[0:128] + (buf[2] + buf[4])
        dst[128:256] = src[128:256] + (buf[3] + buf[5])

    def p_last(n):
        last(n, p1.at[n])
        part_own(0, n, p1.at[n])

    def q_last(n):
        last(4 + n, q1.at[n])
        part_own(1, n, q1.at[n])

    prep_s(0)
    unit(0, 0)
    first(0, 0)
    first(1, 0)
    for d in range(1, 4):
        arrived(gx.at[d - 1], kgx[d - 1])
    gz[3] = (gm[piece(h, y)] + gx[0]) + (gx[1] + gx[2])
    for d in range(1, 4):
        go(gz.at[3], gz.at[d - 1], kgz[d - 1], zn[d])
    first(0, 4, 5)
    prep_s(1)
    unit(0, 1)
    first(0, 1)
    first(1, 1, 4, 5)
    for d in range(1, 4):
        arrived(gz.at[d - 1], kgz[d - 1])
    gb[piece(h, y)] = (gz[3] + gz[0]) + (gz[1] + gz[2])
    for i, (o, d) in enumerate(eight):
        go(gb.at[piece(h, y)], gb.at[piece(h, y)], kgb[i], ts[o], yn[d])
    prep_s(2)
    unit(1, 0)
    first(2, 0)
    first(0, 6, 7)
    second_a(0)
    second_b(0)
    for i, (o, d) in enumerate(eight):
        arrived(gb.at[piece(hs[o], (y + 4 - d) % NY)], kgb[i])
    gw[...] = gb[...]
    eye(li)
    prep_s(3)
    factor(gw, li, FAC[0])
    unit(1, 1)
    first(2, 1)
    first(1, 6, 7)
    second_a(1, 4, 5)
    second_b(1)
    factor(gw, li, FAC[1])
    unit(0, 2)
    first(0, 2)
    first(1, 2)
    first(2, 4, 5)
    second_b(4, 5)
    second_a(6, 7)
    factor(gw, li, FAC[2])
    unit(0, 3)
    first(0, 3)
    first(1, 3)
    p_last(0)
    p_last(1)
    factor(gw, li, FAC[3])
    unit(1, 2)
    first(2, 2, 6, 7)
    second_a(2)
    second_b(2, 6, 7)
    q_last(0)
    q_last(1)
    factor(gw, li, FAC[4])
    unit(1, 3)
    first(2, 3)
    second_a(3)
    second_b(3)
    part_on(0, 1, p1.at[1])
    part_on(1, 1, q1.at[1])
    s_o[...] = s_ext[pl.ds(pl.multiple_of(16 + R * h, 16), R), :]
    li_o[...] = li[...]
    p_last(2)
    part_on(0, 2, p1.at[2])
    q_last(2)
    part_on(1, 2, q1.at[2])
    last(3, p1.at[3])
    last(7, q1.at[3])
    part_sum(0, p1.at[3], raw.at[0])
    part_sum(1, q1.at[3], raw.at[1])

    for c in outs:
        c.wait_send()
    heads[0].wait_send()
    heads[1].wait_send()

    @pl.when(gives)
    def _():
        halos[0].wait_send()
        halos[1].wait_send()


FAC = (range(0, 3), range(3, 6), range(6, 9), range(9, 12), range(12, 16))


def apply_inverse(own, raw, inv, basis, coeffs):
    root = float(NX * NZ * PR) ** 0.5
    basis[...] = lax.dot_general(own[...], inv[...], NT_DOT, precision=HI, preferred_element_type=F32) * root
    for j in range(2):
        coeffs[j] = lax.dot_general(raw[j], inv[...], NT_DOT, precision=HI, preferred_element_type=F32)


def eye(li):
    rows = lax.broadcasted_iota(jnp.int32, (K, K), 0)
    cols = lax.broadcasted_iota(jnp.int32, (K, K), 1)
    li[...] = jnp.where(rows == cols, 1.0, 0.0).astype(F32)


def factor(g, li, blocks):
    for jb in blocks:
        base = 8 * jb
        rows = lax.broadcasted_iota(jnp.int32, (K - base, 1), 0)
        av, bv = g[base:], li[base:]
        for j in range(8):
            at_j = slice(base + j, base + j + 1)
            r = lax.rsqrt(av[j : j + 1, at_j])
            ra, rb = av[j : j + 1] * r, bv[j : j + 1] * r
            f = jnp.where(rows > j, av[:, at_j] * r, 0.0)
            av = av - f * ra
            bv = jnp.where(rows == j, rb, bv - f * rb)
        g[base:] = av
        li[base:] = bv


N_SEM = 4 + 3 + 3 + 4 + 48 + 12 + 7 + 3 + 3 + 7


def on_device(record, test_matrix):
    V = pl.BlockSpec(memory_space=pltpu.VMEM)
    H = pl.BlockSpec(memory_space=pl.ANY)
    own, raw, inv = pl.pallas_call(
        body,
        out_shape=(
            jax.ShapeDtypeStruct((R, K), F32),
            jax.ShapeDtypeStruct((2, CH, K), F32),
            jax.ShapeDtypeStruct((K, K), F32),
        ),
        in_specs=[H, H],
        out_specs=(V, V, V),
        scratch_shapes=[
            pltpu.VMEM((PR + 64, CH), F32),
            pltpu.VMEM((8, A, 2, CH, K), F32),
            pltpu.VMEM((R + 16, KC), BF16),
            pltpu.VMEM((2, KC, 2 * K), BF16),
            pltpu.VMEM((4, R // 2 + 16, K), F32),
            pltpu.VMEM((R, K), F32),
            pltpu.VMEM((3, 256, K), F32),
            pltpu.VMEM((PR + 32, K), F32),
            pltpu.VMEM((A * CH, KT), BF16),
            pltpu.VMEM((4, KT, 2 * K), BF16),
            pltpu.VMEM((8, A * CH, K), F32),
            pltpu.VMEM((8, 6, 128, K), F32),
            pltpu.VMEM((4, CH, K), F32),
            pltpu.VMEM((4, CH, K), F32),
            pltpu.VMEM((6, 128, K), F32),
            pltpu.VMEM((6, 128, K), F32),
            pltpu.VMEM((K, K), F32),
            pltpu.VMEM((7, 16, K), F32),
            pltpu.VMEM((3, 16, K), F32),
            pltpu.VMEM((4, 16, K), F32),
            pltpu.VMEM((K, K), F32),
            pltpu.VMEM((K, K), F32),
            pltpu.VMEM((K, K), F32),
            pltpu.SemaphoreType.DMA((33,)),
            pltpu.SemaphoreType.DMA((N_SEM,)),
            pltpu.SemaphoreType.DMA((N_SEM,)),
        ],
        compiler_params=pltpu.CompilerParams(collective_id=0, has_side_effects=True, vmem_limit_bytes=60 * 2**20),
    )(record, test_matrix)
    return pl.pallas_call(
        apply_inverse,
        out_shape=(jax.ShapeDtypeStruct((R, K), F32), jax.ShapeDtypeStruct((2, CH, K), F32)),
        in_specs=[V, V, V],
        out_specs=(V, V),
    )(own, raw, inv)


def solution(mesh):
    return jax.shard_map(
        on_device,
        mesh=mesh,
        in_specs=(P("tm", "chan"), P(None, "chan", None)),
        out_specs=(P("tm", None), P("tm", "chan", None)),
        check_vma=False,
    )
```
